256 devices in a mesh: section: 16 (over x, z_hi), head: 16 (over y, z_lo, core).
Axes of the slice: x: 4, y: 4, z: 8 (z_hi: 4, z_lo: 2; z = z_hi * 2 + z_lo), core: 2. Of those that a mesh axis runs over, the one named last changes fastest.
Arguments:
- qkv: bfloat16 [16, 288, 3, 6144], P('section', 'head'), may hold values from -160 to 160
- stale_kv: bfloat16 [16, 4608, 2, 6144], P('section', None, None, 'head'), may hold values from -6 to 6
- out_weight: bfloat16 [16, 6144, 6144], P('section', 'head'), may hold values from -0.3125 to 0.3125
- residual: bfloat16 [16, 288, 6144], P('section', 'head'), may hold values from -6 to 6
- gate: float32 [16, 6144], P('section'), may hold values from 0.5 to 2
- patch_of_section: int32 [16], P('section'), may hold values from 0 to 15, each once
Outputs:
- handed: bfloat16 [16, 288, 6144], P('section', 'head')
The draws below stay inside these ranges and needn't reach their ends.
All inputs are finite; a program needn't handle non-finite values.
Results may differ from the reference program's by a relative error of at most 0.023.
Values may be sent and summed in bfloat16 or wider, within the bound.
No kernel may reach another device: no remote copies, remote signals or barrier semaphores. Data moves between devices by JAX's collectives and lax.ppermute only.
A program may use at most 128 MiB of HBM per device.

```python
import math
import jax
import jax.numpy as jnp
from jax import lax

D = 6144
HEADS = 48
HD = 128
PATCH = 288
TOTAL = 4608
N_SECTION = 16
N_HEAD = 16


def draw_qkv(key, part):
    key = jax.random.fold_in(key, 11)
    shape = (N_SECTION, PATCH, 3, HEADS * HD)
    base = jnp.clip(jax.random.normal(key, shape, jnp.float32), -6.0, 6.0)
    factor = jnp.array([2.0, 1.0, 1.0], jnp.float32)[None, None, :, None]
    drawn = base * factor
    return drawn.astype(jnp.bfloat16)


def levels(rng, extent, cuts, smallest, high):
    def one(dim, blocks):
        steps = jax.random.uniform(jax.random.fold_in(jax.random.fold_in(rng, 6), dim), (blocks,), jnp.float32, smallest / len(cuts), high / len(cuts))
        return jnp.repeat(jnp.exp(steps), extent[dim] // blocks).reshape((-1,) + (1,) * (len(extent) - dim - 1))

    factor_of = one(*cuts[0])
    for cut in cuts[1:]:
        factor_of = factor_of * one(*cut)
    return factor_of


def gaussian(own_key, shape, deviation, reach, split=(), dtype=jnp.bfloat16):
    gain = levels(own_key, shape, split, -0.22, 0.18) if split else 1.0
    result = jax.random.normal(own_key, shape, jnp.float32) * deviation * gain
    return jnp.minimum(jnp.maximum(result, -reach), reach).astype(dtype)


def setup_inputs(seed: int = 0) -> dict:
    splits = jax.random.split(jax.random.key(seed), 7)
    qkv = draw_qkv(jax.random.fold_in(splits[6], 71), 0)
    stale_kv = gaussian(splits[1], (N_SECTION, TOTAL, 2, HEADS * HD), 1.0, 6.0, ((0, 16), (3, 16)))
    out_weight = gaussian(splits[2], (N_SECTION, HEADS * HD, D), (HEADS * HD // 16) ** -0.5, 0.3125, ((0, 16), (1, 16)))
    residual = gaussian(splits[3], (N_SECTION, PATCH, D), 1.0, 6.0, ((0, 16), (1, 16)))
    gate = jnp.clip(jnp.exp(math.log(2.0) - 1.3862944 * jax.random.uniform(splits[4], (N_SECTION, D), jnp.float32) ** levels(splits[4], (N_SECTION, D), ((0, 16),), -0.2, 0.2)), 0.5, 2.0)
    patch_of_section = jax.random.permutation(splits[5], N_SECTION).astype(jnp.int32)
    return dict(qkv=qkv, stale_kv=stale_kv, out_weight=out_weight, residual=residual, gate=gate, patch_of_section=patch_of_section)


def one_section(operands):
    fresh, history, out_rows, stream, gating, patch_index = operands
    own_start = (patch_index * PATCH).astype(jnp.int32)
    merged_kv = lax.dynamic_update_slice(history, fresh[:, 1:3, :], (own_start, jnp.int32(0), jnp.int32(0)))
    queries = fresh[:, 0, :].reshape(PATCH, HEADS, HD).astype(jnp.float32)
    keys_all = merged_kv[:, 0, :].reshape(TOTAL, HEADS, HD).astype(jnp.float32)
    values_all = merged_kv[:, 1, :].reshape(TOTAL, HEADS, HD).astype(jnp.float32)
    scores = jnp.einsum("qhd,khd->hqk", queries, keys_all) * (1.0 / (HD ** 0.5))
    highest = jnp.max(scores, axis=-1, keepdims=True)
    expon = jnp.exp(scores - highest)
    probs = (expon / jnp.sum(expon, axis=-1, keepdims=True)).astype(jnp.bfloat16)
    attended = jnp.einsum("hqk,khd->qhd", probs.astype(jnp.float32), values_all)
    attended = attended.astype(jnp.bfloat16).reshape(PATCH, N_HEAD, (HEADS // N_HEAD) * HD)
    grouped_rows = out_rows.reshape(N_HEAD, (HEADS // N_HEAD) * HD, D)
    group_sums = jnp.einsum("qgc,gcd->gqd", attended.astype(jnp.float32), grouped_rows.astype(jnp.float32))
    group_sums = lax.optimization_barrier(group_sums.astype(jnp.bfloat16))
    projected = jnp.sum(group_sums.astype(jnp.float32), axis=0)
    return (stream.astype(jnp.float32) + gating[None, :] * projected).astype(jnp.bfloat16)


def reference(qkv, stale_kv, out_weight, residual, gate, patch_of_section):
    updated = lax.map(one_section, (qkv, stale_kv, out_weight, residual, gate, patch_of_section))
    return jnp.roll(updated, 1, axis=0)
```

```python
import functools
import math

import jax
import jax.numpy as jnp
from jax import lax
from jax.experimental import pallas as pl
from jax.experimental.pallas import tpu as pltpu
from jax.sharding import PartitionSpec as P

HD = 128
CORES = 2
MAIN = 16
VMEM_LIMIT = 56 * 2**20


def attend_kernel(scalars, arrived, kv, keep, send, q_s, fresh_s, kv_s, sems, *, heads, chunk):
    groups = arrived.shape[0]
    tok = arrived.shape[1] // 3
    half = tok * groups // CORES
    peers = groups // CORES
    keys = kv.shape[1]
    patch = tok * groups
    rest = tok - MAIN
    scale = math.log2(math.e) / math.sqrt(HD)
    copies = []
    for h in range(heads):
        for t in range(2):
            cols = pl.ds(h * HD, HD)
            copy = pltpu.make_async_copy(
                kv.at[t, :, cols], kv_s.at[t, :, cols], sems.at[2 * h + t]
            )
            copy.start()
            copies.append(copy)
    core = scalars[1]
    for side in range(CORES):
        which = core if side == 0 else 1 - core
        for k in range(peers):
            block = arrived[CORES * k + which]
            for t in range(3):
                target = q_s if t == 0 else fresh_s.at[t - 1]
                rows = block[t * tok : (t + 1) * tok]
                target[pl.ds(side * half + MAIN * k, MAIN), :] = rows[:MAIN]
                target[pl.ds(side * half + MAIN * peers + rest * k, rest), :] = rows[MAIN:]
    own = pl.multiple_of(scalars[0] * patch, MAIN)
    for h in range(heads):
        cols = slice(h * HD, (h + 1) * HD)
        for t in range(2):
            copies[2 * h + t].wait()
            kv_s[t, pl.ds(own, patch), cols] = fresh_s[t, :, cols]
        q = q_s[:, cols]

        def score(j):
            k = kv_s[0, chunk * j : chunk * (j + 1), cols]
            return lax.dot_general(
                q, k, (((1,), (1,)), ((), ())), preferred_element_type=jnp.float32
            )

        top = total = acc = None
        upcoming = score(0)
        for j in range(keys // chunk):
            s = upcoming
            if j + 1 < keys // chunk:
                upcoming = score(j + 1)
            high = jnp.max(s, axis=1, keepdims=True)
            new_top = high if j == 0 else jnp.maximum(top, high)
            p = jnp.exp2((s - new_top) * scale)
            part = jnp.sum(p, axis=1, keepdims=True)
            v = kv_s[1, chunk * j : chunk * (j + 1), cols]
            out = jnp.dot(p.astype(jnp.bfloat16), v, preferred_element_type=jnp.float32)
            if j == 0:
                total, acc = part, out
            else:
                fade = jnp.exp2((top - new_top) * scale)
                total = total * fade + part
                acc = acc * fade + out
            top = new_top
        done = (acc / total).astype(jnp.bfloat16)
        keep[:, cols] = done[:half]
        send[:, cols] = done[half:]


def attend(scalars, arrived, kv):
    groups, rows, width = arrived.shape
    heads = width // HD
    keys = kv.shape[1]
    patch = rows // 3 * groups
    result = jax.ShapeDtypeStruct((patch // CORES, width), jnp.bfloat16)
    vmem = pl.BlockSpec(memory_space=pltpu.VMEM)
    return pl.pallas_call(
        functools.partial(attend_kernel, heads=heads, chunk=keys // 6),
        in_specs=[pl.BlockSpec(memory_space=pltpu.SMEM), vmem, pl.BlockSpec(memory_space=pl.ANY)],
        out_specs=[vmem, vmem],
        out_shape=[result, result],
        scratch_shapes=[
            pltpu.VMEM((patch, width), jnp.bfloat16),
            pltpu.VMEM((2, patch, width), jnp.bfloat16),
            pltpu.VMEM((2, keys, width), jnp.bfloat16),
            pltpu.SemaphoreType.DMA((2 * heads,)),
        ],
        compiler_params=pltpu.CompilerParams(vmem_limit_bytes=VMEM_LIMIT),
        name="attend",
    )(scalars, arrived, kv)


def project_kernel(keep, other, w_keep, w_other, out, rest_s, *, cuts, peers, per_step):
    step = pl.program_id(0)
    rest = keep.shape[0] // peers - MAIN
    width = out.shape[2] // per_step
    y = jnp.dot(keep[...], w_keep[...], preferred_element_type=jnp.float32)
    y = y + jnp.dot(other[...], w_other[...], preferred_element_type=jnp.float32)
    for d in range(peers):
        out[d] = y[MAIN * d : MAIN * (d + 1)].astype(jnp.bfloat16)
    for b in range(per_step):
        for d in range(peers):
            for t in range(rest):
                row = MAIN * peers + rest * d + t
                value = y[row : row + 1, width * b : width * (b + 1)]
                for s in range(cuts // per_step + 1):
                    cut = s * per_step + b
                    if cut < cuts:

                        @pl.when(step == s)
                        def _():
                            rest_s[d, cuts * t + cut : cuts * t + cut + 1, :] = value

    last = cuts % per_step

    @pl.when(step == cuts // per_step)
    def _():
        for d in range(peers):
            out[d, :, width * last : width * (last + 1)] = rest_s[d].astype(jnp.bfloat16)


def project(keep, other, w_keep, w_other, peers):
    rows, width = keep.shape
    columns = w_keep.shape[1]
    rest = rows // peers - MAIN
    cuts = MAIN // rest
    cut = columns // cuts
    per_step = 3
    steps = cuts // per_step + 1
    whole = pl.BlockSpec((rows, width), lambda i: (0, 0))
    weights = pl.BlockSpec((width, per_step * cut), lambda i: (0, i))
    return pl.pallas_call(
        functools.partial(project_kernel, cuts=cuts, peers=peers, per_step=per_step),
        grid=(steps,),
        in_specs=[whole, whole, weights, weights],
        out_specs=pl.BlockSpec((peers, MAIN, per_step * cut), lambda i: (0, 0, i)),
        out_shape=jax.ShapeDtypeStruct((peers, MAIN, columns + cut), jnp.bfloat16),
        scratch_shapes=[pltpu.VMEM((peers, MAIN, cut), jnp.float32)],
        compiler_params=pltpu.CompilerParams(vmem_limit_bytes=VMEM_LIMIT),
        name="project",
    )(keep, other, w_keep, w_other)


def update_kernel(parts, residual, residual_rest, gate, gate_rest, out):
    columns = residual.shape[1]
    total = parts[0].astype(jnp.float32)
    for d in range(1, parts.shape[0]):
        total = total + parts[d].astype(jnp.float32)
    main = residual[0:MAIN, :].astype(jnp.float32) + gate[...] * total[:, :columns]
    out[:, :columns] = main.astype(jnp.bfloat16)
    tail = residual_rest[...].astype(jnp.float32) + gate_rest[...] * total[:, columns:]
    out[:, columns:] = tail.astype(jnp.bfloat16)


def update(parts, residual, residual_rest, gate, gate_rest):
    vmem = pl.BlockSpec(memory_space=pltpu.VMEM)
    return pl.pallas_call(
        update_kernel,
        in_specs=[vmem] * 5,
        out_specs=vmem,
        out_shape=jax.ShapeDtypeStruct(parts.shape[1:], jnp.bfloat16),
        compiler_params=pltpu.CompilerParams(vmem_limit_bytes=VMEM_LIMIT),
        name="update",
    )(parts, residual, residual_rest, gate, gate_rest)


def unpack_kernel(packed, out):
    rows, columns = out.shape
    rest = rows - MAIN
    cuts = MAIN // rest
    cut = columns // cuts
    out[0:MAIN, :] = packed[:, :columns]
    tail = packed[:, columns:].astype(jnp.float32)
    for b in range(cuts):
        pieces = [tail[cuts * t + b : cuts * t + b + 1] for t in range(rest)]
        out[MAIN:rows, b * cut : (b + 1) * cut] = jnp.concatenate(pieces, axis=0).astype(
            jnp.bfloat16
        )


def unpack(packed, rows, columns):
    vmem = pl.BlockSpec(memory_space=pltpu.VMEM)
    return pl.pallas_call(
        unpack_kernel,
        in_specs=[vmem],
        out_specs=vmem,
        out_shape=jax.ShapeDtypeStruct((rows, columns), jnp.bfloat16),
        name="unpack",
    )(packed)


def shards(qkv, stale_kv, out_weight, residual, gate, patch_of_section):
    groups = lax.axis_size("head")
    sections = lax.axis_size("section")
    peers = groups // CORES
    tok = qkv.shape[1]
    rest = tok - MAIN
    cuts = MAIN // rest
    width = stale_kv.shape[3]
    columns = out_weight.shape[2]
    swap = [(i, i ^ 1) for i in range(groups)]
    same_core = [[CORES * k + c for k in range(peers)] for c in range(CORES)]

    core = lax.axis_index("head") % CORES
    scalars = jnp.stack([patch_of_section[0], core.astype(jnp.int32)])
    blocked = (
        qkv[0].reshape(tok, 3, groups, width).transpose(2, 1, 0, 3).reshape(groups, 3 * tok, width)
    )
    arrived = lax.all_to_all(blocked, "head", split_axis=0, concat_axis=0, tiled=True)
    weight = out_weight[0]
    weight_other = lax.ppermute(weight, "head", swap)
    kv = jnp.transpose(stale_kv[0], (1, 0, 2))
    residual_rest = residual[0, MAIN:].reshape(MAIN, columns // cuts)
    gate_rest = jnp.tile(gate[0].reshape(cuts, columns // cuts), (rest, 1))

    keep, send = attend(scalars, arrived, kv)
    other = lax.ppermute(send, "head", swap)
    partial_sums = project(keep, other, weight, weight_other, peers)
    parts = lax.all_to_all(
        partial_sums, "head", split_axis=0, concat_axis=0, tiled=True, axis_index_groups=same_core
    )
    updated = update(parts, residual[0], residual_rest, gate, gate_rest)
    handed = lax.ppermute(
        updated, "section", [(i, (i + 1) % sections) for i in range(sections)]
    )
    return unpack(handed, tok, columns)[None]


def solution(mesh):
    placed = (
        P("section", "head", None, None),
        P("section", None, None, "head"),
        P("section", "head", None),
        P("section", "head", None),
        P("section", None),
        P("section"),
    )
    return jax.shard_map(
        shards, mesh=mesh, in_specs=placed, out_specs=P("section", "head", None), check_vma=False
    )
```

```python
import functools
import math

import jax
import jax.numpy as jnp
from jax import lax
from jax.experimental import pallas as pl
from jax.experimental.pallas import tpu as pltpu
from jax.sharding import PartitionSpec as P

HD = 128
CORES = 2
MAIN = 16
SPLIT = (1,)
CHUNKS = 6
ATTEND_VMEM = 36 * 2**20
VMEM_LIMIT = 8 * 2**20


def in_vmem(x):
    return pltpu.with_memory_space_constraint(x, pltpu.VMEM)


def in_hbm(x):
    return pltpu.with_memory_space_constraint(x, pltpu.HBM)


def pack_kernel(qkv, out, rows_s):
    tok = qkv.shape[1]
    width = out.shape[2]
    for i in range(tok):
        value = qkv[0, i].astype(jnp.float32)
        for t in range(3):
            rows_s[t * tok + i : t * tok + i + 1, :] = value[t : t + 1]
    for g in range(out.shape[0]):
        out[g] = rows_s[:, g * width : (g + 1) * width].astype(jnp.bfloat16)


def pack(qkv, groups):
    _, tok, _, columns = qkv.shape
    vmem = pl.BlockSpec(memory_space=pltpu.VMEM)
    return pl.pallas_call(
        pack_kernel,
        in_specs=[vmem],
        out_specs=vmem,
        out_shape=jax.ShapeDtypeStruct((groups, 3 * tok, columns // groups), jnp.bfloat16),
        scratch_shapes=[pltpu.VMEM((3 * tok, columns), jnp.float32)],
        compiler_params=pltpu.CompilerParams(vmem_limit_bytes=VMEM_LIMIT),
        name="pack",
    )(qkv)


def stream_kernel(residual, gate, *packed, chunks):
    rest = residual.shape[0] - MAIN
    cuts = MAIN // rest
    stream = residual[...].astype(jnp.float32)
    gates = gate[...]
    for i, (start, size) in enumerate(chunks):
        res_out, gate_out = packed[2 * i : 2 * i + 2]
        cut = size // cuts
        res_out[:, :size] = stream[:MAIN, start : start + size]
        gate_out[:, :size] = jnp.broadcast_to(gates[:, start : start + size], (MAIN, size))
        for b in range(cuts):
            cols = slice(start + b * cut, start + (b + 1) * cut)
            for t in range(rest):
                row = cuts * t + b
                res_out[row : row + 1, size:] = stream[MAIN + t : MAIN + t + 1, cols]
                gate_out[row : row + 1, size:] = gates[:, cols]


def stream(residual, gate, chunks):
    vmem = pl.BlockSpec(memory_space=pltpu.VMEM)
    packed = []
    for _, size in chunks:
        packed += [pltpu.VMEM((MAIN, packed_width(size, residual.shape[0])), jnp.float32)] * 2
    return pl.pallas_call(
        functools.partial(stream_kernel, chunks=chunks),
        in_specs=[vmem, vmem],
        out_specs=[vmem] * len(packed),
        out_shape=packed,
        compiler_params=pltpu.CompilerParams(vmem_limit_bytes=VMEM_LIMIT),
        name="stream",
    )(residual, gate)


def attend_kernel(
    scalars, arrived, kv, w_keep, w_other, keep, send, w_out, q_s, fresh_s, sems, *kv_s, heads, chunk
):
    copies = []
    for h in range(heads):
        for t in range(2):
            copies.append(
                pltpu.make_async_copy(
                    kv.at[t, :, pl.ds(h * HD, HD)], kv_s[2 * h + t], sems.at[2 * h + t]
                )
            )
    for i, w in enumerate((w_keep, w_other)):
        copies.append(pltpu.make_async_copy(w, w_out.at[i], sems.at[2 * heads + i]))
    for copy in copies:
        copy.start()
    groups = arrived.shape[0]
    tok = arrived.shape[1] // 3
    half = tok * groups // CORES
    peers = groups // CORES
    patch = tok * groups
    rest = tok - MAIN
    scale = math.log2(math.e) / math.sqrt(HD)
    core = scalars[1]
    for side in range(CORES):
        which = core if side == 0 else 1 - core
        for k in range(peers):
            block = arrived[CORES * k + which]
            for t in range(3):
                target = q_s if t == 0 else fresh_s.at[t - 1]
                rows = block[t * tok : (t + 1) * tok]
                target[pl.ds(side * half + MAIN * k, MAIN), :] = rows[:MAIN]
                target[pl.ds(side * half + MAIN * peers + rest * k, rest), :] = rows[MAIN:]
    own = pl.ds(pl.multiple_of(scalars[0] * patch, MAIN), patch)

    def ready(h, t):
        copies[2 * h + t].wait()
        kv_s[2 * h + t][own, :] = fresh_s[t, :, h * HD : (h + 1) * HD]

    keys = kv_s[0].shape[0]
    for h in range(heads):
        ready(h, 0)
        ready(h, 1)
        cols = slice(h * HD, (h + 1) * HD)
        q = q_s[:, cols]

        def score(j):
            k = kv_s[2 * h][j * chunk : (j + 1) * chunk, :]
            return lax.dot_general(
                q, k, (((1,), (1,)), ((), ())), preferred_element_type=jnp.float32
            )

        top = total = acc = None
        upcoming = score(0)
        for j in range(keys // chunk):
            s = upcoming
            if j + 1 < keys // chunk:
                upcoming = score(j + 1)
            high = jnp.max(s, axis=1, keepdims=True)
            new_top = high if j == 0 else jnp.maximum(top, high)
            p = jnp.exp2((s - new_top) * scale)
            part = jnp.sum(p, axis=1, keepdims=True)
            v = kv_s[2 * h + 1][j * chunk : (j + 1) * chunk, :]
            out = jnp.dot(p.astype(jnp.bfloat16), v, preferred_element_type=jnp.float32)
            if j == 0:
                total, acc = part, out
            else:
                fade = jnp.exp2((top - new_top) * scale)
                total = total * fade + part
                acc = acc * fade + out
            top = new_top
        done = (acc / total).astype(jnp.bfloat16)
        keep[:, cols] = done[:half]
        send[:, cols] = done[half:]
    for copy in copies[2 * heads :]:
        copy.wait()


def attend(scalars, arrived, kv, w_keep, w_other):
    groups, rows, width = arrived.shape
    keys = kv.shape[1]
    heads = width // HD
    patch = rows // 3 * groups
    result = pltpu.VMEM((patch // CORES, width), jnp.bfloat16)
    vmem = pl.BlockSpec(memory_space=pltpu.VMEM)
    anywhere = pl.BlockSpec(memory_space=pl.ANY)
    return pl.pallas_call(
        functools.partial(attend_kernel, heads=heads, chunk=keys // CHUNKS),
        in_specs=[pl.BlockSpec(memory_space=pltpu.SMEM), vmem] + [anywhere] * 3,
        out_specs=[vmem] * 3,
        out_shape=[
            result,
            result,
            pltpu.VMEM((CORES,) + w_keep.shape, w_keep.dtype),
        ],
        scratch_shapes=[
            pltpu.VMEM((patch, width), jnp.bfloat16),
            pltpu.VMEM((2, patch, width), jnp.bfloat16),
            pltpu.SemaphoreType.DMA((2 * heads + 2,)),
        ]
        + [pltpu.VMEM((keys, HD), jnp.bfloat16)] * (2 * heads),
        compiler_params=pltpu.CompilerParams(vmem_limit_bytes=ATTEND_VMEM),
        name="attend",
    )(scalars, in_vmem(arrived), *map(in_hbm, (kv, w_keep, w_other)))


def packed_width(size, tok):
    return size * tok // MAIN


def project_kernel(keep, other, weights, out, rest_s, *, start, size):
    peers = out.shape[0]
    cut = out.shape[2] - size
    cuts = size // cut
    rest = MAIN // cuts
    both = jnp.concatenate([keep[...], other[...]], axis=1)
    for b in range(cuts):
        cols = slice(start + b * cut, start + (b + 1) * cut)
        w = jnp.concatenate([weights[i, :, cols] for i in range(CORES)], axis=0)
        y = jnp.dot(both, w, preferred_element_type=jnp.float32)
        for d in range(peers):
            rows = y[MAIN * d : MAIN * (d + 1)]
            out[d, :, b * cut : (b + 1) * cut] = rows.astype(jnp.bfloat16)
            for t in range(rest):
                row = MAIN * peers + rest * d + t
                rest_s[d, cuts * t + b : cuts * t + b + 1, :] = y[row : row + 1]
    for d in range(peers):
        out[d, :, size:] = rest_s[d].astype(jnp.bfloat16)


def project(keep, other, weights, peers, start, size):
    rows, _ = keep.shape
    width = packed_width(size, rows // peers)
    vmem = pl.BlockSpec(memory_space=pltpu.VMEM)
    return pl.pallas_call(
        functools.partial(project_kernel, start=start, size=size),
        in_specs=[vmem] * 3,
        out_specs=vmem,
        out_shape=pltpu.VMEM((peers, MAIN, width), jnp.bfloat16),
        scratch_shapes=[pltpu.VMEM((peers, MAIN, width - size), jnp.float32)],
        compiler_params=pltpu.CompilerParams(vmem_limit_bytes=VMEM_LIMIT),
        name=f"project_{start}",
    )(in_vmem(keep), in_vmem(other), in_vmem(weights))


def update_kernel(parts, residual, gate, out):
    total = parts[0].astype(jnp.float32)
    for d in range(1, parts.shape[0]):
        total = total + parts[d].astype(jnp.float32)
    out[...] = (residual[...] + gate[...] * total).astype(jnp.bfloat16)


def update(parts, residual, gate):
    vmem = pl.BlockSpec(memory_space=pltpu.VMEM)
    return pl.pallas_call(
        update_kernel,
        in_specs=[vmem] * 3,
        out_specs=vmem,
        out_shape=pltpu.VMEM(parts.shape[1:], jnp.bfloat16),
        compiler_params=pltpu.CompilerParams(vmem_limit_bytes=VMEM_LIMIT),
        name="update",
    )(in_vmem(parts), in_vmem(residual), in_vmem(gate))


def unpack_kernel(*refs, chunks):
    out = refs[-1]
    rest = out.shape[0] - MAIN
    cuts = MAIN // rest
    for packed, (start, size) in zip(refs, chunks):
        cut = size // cuts
        out[0:MAIN, start : start + size] = packed[:, :size]
        tail = packed[:, size:].astype(jnp.float32)
        for b in range(cuts):
            pieces = [tail[cuts * t + b : cuts * t + b + 1] for t in range(rest)]
            cols = slice(start + b * cut, start + (b + 1) * cut)
            out[MAIN:, cols] = jnp.concatenate(pieces, axis=0).astype(jnp.bfloat16)


def unpack(packed, rows, columns, chunks):
    vmem = pl.BlockSpec(memory_space=pltpu.VMEM)
    return pl.pallas_call(
        functools.partial(unpack_kernel, chunks=chunks),
        in_specs=[vmem] * len(packed),
        out_specs=vmem,
        out_shape=jax.ShapeDtypeStruct((rows, columns), jnp.bfloat16),
        compiler_params=pltpu.CompilerParams(vmem_limit_bytes=VMEM_LIMIT),
        name="unpack",
    )(*map(in_vmem, packed))


def shards(qkv, stale_kv, out_weight, residual, gate, patch_of_section):
    groups = lax.axis_size("head")
    sections = lax.axis_size("section")
    peers = groups // CORES
    tok = qkv.shape[1]
    columns = out_weight.shape[2]
    swap = [(i, i ^ 1) for i in range(groups)]
    same_core = [[CORES * k + c for k in range(peers)] for c in range(CORES)]
    chunks = []
    for parts in SPLIT:
        start = sum(size for _, size in chunks)
        chunks.append((start, columns * parts // sum(SPLIT)))

    core = lax.axis_index("head") % CORES
    scalars = jnp.stack([patch_of_section[0], core.astype(jnp.int32)])
    weight = out_weight[0]
    weight_other = lax.ppermute(weight, "head", swap)
    blocked = pack(qkv, groups)
    arrived = lax.all_to_all(blocked, "head", split_axis=0, concat_axis=0, tiled=True)
    kv = jnp.transpose(stale_kv[0], (1, 0, 2))

    keep, send, weights = attend(scalars, arrived, kv, weight, weight_other)
    other = lax.ppermute(send, "head", swap)
    packed = stream(residual[0], gate, chunks)
    handed = []
    for i, (start, size) in enumerate(chunks):
        sums = project(keep, other, weights, peers, start, size)
        parts = lax.all_to_all(
            sums, "head", split_axis=0, concat_axis=0, tiled=True, axis_index_groups=same_core
        )
        updated = update(parts, packed[2 * i], packed[2 * i + 1])
        handed.append(
            lax.ppermute(updated, "section", [(j, (j + 1) % sections) for j in range(sections)])
        )
    return unpack(handed, tok, columns, chunks)[None]


def solution(mesh):
    placed = (
        P("section", "head", None, None),
        P("section", None, None, "head"),
        P("section", "head", None),
        P("section", "head", None),
        P("section", None),
        P("section"),
    )
    return jax.shard_map(
        shards, mesh=mesh, in_specs=placed, out_specs=P("section", "head", None), check_vma=False
    )
```

```python
import functools
import math

import jax
import jax.numpy as jnp
from jax import lax
from jax.experimental import pallas as pl
from jax.experimental.pallas import tpu as pltpu
from jax.sharding import PartitionSpec as P

HD = 128
CORES = 2
MAIN = 16
SPLIT = (1,)
CHUNKS = 6
ATTEND_VMEM = 36 * 2**20
VMEM_LIMIT = 8 * 2**20


def in_vmem(x):
    return pltpu.with_memory_space_constraint(x, pltpu.VMEM)


def in_hbm(x):
    return pltpu.with_memory_space_constraint(x, pltpu.HBM)


def pack_kernel(qkv, out, in_s, rows_s, out_s, in_sems, out_sems, *, pieces):
    tok = qkv.shape[1]
    groups, _, width = out.shape
    part = tok // pieces
    step = groups // pieces_out(groups)
    arriving = []
    for n in range(pieces):
        rows = pl.ds(n * part, part)
        arriving.append(pltpu.make_async_copy(qkv.at[0, rows], in_s.at[rows], in_sems.at[n]))
        arriving[-1].start()
    for n in range(pieces):
        arriving[n].wait()
        for i in range(n * part, (n + 1) * part):
            value = in_s[i].astype(jnp.float32)
            for t in range(3):
                rows_s[t * tok + i : t * tok + i + 1, :] = value[t : t + 1]
    leaving = []
    for n in range(pieces_out(groups)):
        for g in range(n * step, (n + 1) * step):
            out_s[g] = rows_s[:, g * width : (g + 1) * width].astype(jnp.bfloat16)
        some = pl.ds(n * step, step)
        leaving.append(pltpu.make_async_copy(out_s.at[some], out.at[some], out_sems.at[n]))
        leaving[-1].start()
    for copy in leaving:
        copy.wait()


def pieces_out(groups):
    return 4 if groups % 4 == 0 else 1


def pack(qkv, groups):
    _, tok, _, columns = qkv.shape
    shape = (groups, 3 * tok, columns // groups)
    pieces = 3 if tok % 3 == 0 else 1
    anywhere = pl.BlockSpec(memory_space=pl.ANY)
    return pl.pallas_call(
        functools.partial(pack_kernel, pieces=pieces),
        in_specs=[anywhere],
        out_specs=anywhere,
        out_shape=pltpu.HBM(shape, jnp.bfloat16),
        scratch_shapes=[
            pltpu.VMEM((tok, 3, columns), jnp.bfloat16),
            pltpu.VMEM((3 * tok, columns), jnp.float32),
            pltpu.VMEM(shape, jnp.bfloat16),
            pltpu.SemaphoreType.DMA((pieces,)),
            pltpu.SemaphoreType.DMA((pieces_out(groups),)),
        ],
        compiler_params=pltpu.CompilerParams(vmem_limit_bytes=VMEM_LIMIT),
        name="pack",
    )(in_hbm(qkv))


def stream_kernel(residual, gate, *packed, chunks):
    rest = residual.shape[0] - MAIN
    cuts = MAIN // rest
    stream = residual[...].astype(jnp.float32)
    gates = gate[...]
    for i, (start, size) in enumerate(chunks):
        res_out, gate_out = packed[2 * i : 2 * i + 2]
        cut = size // cuts
        res_out[:, :size] = stream[:MAIN, start : start + size]
        gate_out[:, :size] = jnp.broadcast_to(gates[:, start : start + size], (MAIN, size))
        for b in range(cuts):
            cols = slice(start + b * cut, start + (b + 1) * cut)
            for t in range(rest):
                row = cuts * t + b
                res_out[row : row + 1, size:] = stream[MAIN + t : MAIN + t + 1, cols]
                gate_out[row : row + 1, size:] = gates[:, cols]


def stream(residual, gate, chunks):
    vmem = pl.BlockSpec(memory_space=pltpu.VMEM)
    packed = []
    for _, size in chunks:
        packed += [pltpu.VMEM((MAIN, packed_width(size, residual.shape[0])), jnp.float32)] * 2
    return pl.pallas_call(
        functools.partial(stream_kernel, chunks=chunks),
        in_specs=[vmem, vmem],
        out_specs=[vmem] * len(packed),
        out_shape=packed,
        compiler_params=pltpu.CompilerParams(vmem_limit_bytes=VMEM_LIMIT),
        name="stream",
    )(residual, gate)


def prefetch_kernel(kv, out, sems):
    copies = []
    for t in range(2):
        copies.append(pltpu.make_async_copy(kv.at[t, :, pl.ds(0, HD)], out.at[t], sems.at[t]))
        copies[-1].start()
    for copy in copies:
        copy.wait()


def prefetch(kv):
    return pl.pallas_call(
        prefetch_kernel,
        in_specs=[pl.BlockSpec(memory_space=pl.ANY)],
        out_specs=pl.BlockSpec(memory_space=pltpu.VMEM),
        out_shape=pltpu.VMEM((2, kv.shape[1], HD), kv.dtype),
        scratch_shapes=[pltpu.SemaphoreType.DMA((2,))],
        compiler_params=pltpu.CompilerParams(vmem_limit_bytes=2**20),
        name="prefetch",
    )(in_hbm(kv))


def attend_kernel(
    scalars, arrived, first_in, kv, w_keep, w_other,
    keep, send, w_out, first, q_s, fresh_s, sems, *kv_s, heads, chunk
):
    copies = []
    kv_s = (first.at[0], first.at[1]) + kv_s
    for h in range(1, heads):
        for t in range(2):
            n = 2 * (h - 1) + t
            copies.append(
                pltpu.make_async_copy(kv.at[t, :, pl.ds(h * HD, HD)], kv_s[2 * h + t], sems.at[n])
            )
    for i, w in enumerate((w_keep, w_other)):
        copies.append(pltpu.make_async_copy(w, w_out.at[i], sems.at[2 * heads - 2 + i]))
    for copy in copies:
        copy.start()
    groups = arrived.shape[0]
    tok = arrived.shape[1] // 3
    half = tok * groups // CORES
    peers = groups // CORES
    patch = tok * groups
    rest = tok - MAIN
    scale = math.log2(math.e) / math.sqrt(HD)
    core = scalars[1]
    for side in range(CORES):
        which = core if side == 0 else 1 - core
        for k in range(peers):
            block = arrived[CORES * k + which]
            for t in range(3):
                target = q_s if t == 0 else fresh_s.at[t - 1]
                rows = block[t * tok : (t + 1) * tok]
                target[pl.ds(side * half + MAIN * k, MAIN), :] = rows[:MAIN]
                target[pl.ds(side * half + MAIN * peers + rest * k, rest), :] = rows[MAIN:]
    own = pl.ds(pl.multiple_of(scalars[0] * patch, MAIN), patch)

    def ready(h, t):
        if h > 0:
            copies[2 * (h - 1) + t].wait()
        kv_s[2 * h + t][own, :] = fresh_s[t, :, h * HD : (h + 1) * HD]

    keys = kv_s[0].shape[0]
    for h in range(heads):
        ready(h, 0)
        ready(h, 1)
        cols = slice(h * HD, (h + 1) * HD)
        q = q_s[:, cols]

        def score(j):
            k = kv_s[2 * h][j * chunk : (j + 1) * chunk, :]
            return lax.dot_general(
                q, k, (((1,), (1,)), ((), ())), preferred_element_type=jnp.float32
            )

        top = total = acc = None
        upcoming = score(0)
        for j in range(keys // chunk):
            s = upcoming
            if j + 1 < keys // chunk:
                upcoming = score(j + 1)
            high = jnp.max(s, axis=1, keepdims=True)
            new_top = high if j == 0 else jnp.maximum(top, high)
            p = jnp.exp2((s - new_top) * scale)
            v = kv_s[2 * h + 1][j * chunk : (j + 1) * chunk, :]
            v = jnp.concatenate([v, jnp.ones_like(v)], axis=1)
            out = jnp.dot(p.astype(jnp.bfloat16), v, preferred_element_type=jnp.float32)
            out, part = out[:, :HD], out[:, HD:]
            if j == 0:
                total, acc = part, out
            else:
                fade = jnp.exp2((top - new_top) * scale)
                total = total * fade + part
                acc = acc * fade + out
            top = new_top
        done = (acc / total).astype(jnp.bfloat16)
        keep[:, cols] = done[:half]
        send[:, cols] = done[half:]
    for copy in copies[2 * heads - 2 :]:
        copy.wait()


def attend(scalars, arrived, first, kv, w_keep, w_other):
    groups, rows, width = arrived.shape
    keys = kv.shape[1]
    heads = width // HD
    patch = rows // 3 * groups
    result = pltpu.VMEM((patch // CORES, width), jnp.bfloat16)
    vmem = pl.BlockSpec(memory_space=pltpu.VMEM)
    anywhere = pl.BlockSpec(memory_space=pl.ANY)
    return pl.pallas_call(
        functools.partial(attend_kernel, heads=heads, chunk=keys // CHUNKS),
        in_specs=[pl.BlockSpec(memory_space=pltpu.SMEM), vmem, vmem] + [anywhere] * 3,
        out_specs=[vmem] * 4,
        out_shape=[
            result,
            result,
            pltpu.VMEM((CORES,) + w_keep.shape, w_keep.dtype),
            pltpu.VMEM(first.shape, first.dtype),
        ],
        scratch_shapes=[
            pltpu.VMEM((patch, width), jnp.bfloat16),
            pltpu.VMEM((2, patch, width), jnp.bfloat16),
            pltpu.SemaphoreType.DMA((2 * heads,)),
        ]
        + [pltpu.VMEM((keys, HD), jnp.bfloat16)] * (2 * heads - 2),
        input_output_aliases={2: 3},
        compiler_params=pltpu.CompilerParams(vmem_limit_bytes=ATTEND_VMEM),
        name="attend",
    )(scalars, in_vmem(arrived), in_vmem(first), *map(in_hbm, (kv, w_keep, w_other)))


def packed_width(size, tok):
    return size * tok // MAIN


def project_kernel(keep, other, weights, out, out_s, rest_s, sems, *, start, size):
    peers = out.shape[0]
    cut = out.shape[2] - size
    cuts = size // cut
    rest = MAIN // cuts
    both = jnp.concatenate([keep[...], other[...]], axis=1)
    copies = []

    def leave(b):
        cols = pl.ds(b * cut, cut)
        copies.append(pltpu.make_async_copy(out_s.at[:, :, cols], out.at[:, :, cols], sems.at[b]))
        copies[-1].start()

    for b in range(cuts):
        cols = slice(start + b * cut, start + (b + 1) * cut)
        w = jnp.concatenate([weights[i, :, cols] for i in range(CORES)], axis=0)
        y = jnp.dot(both, w, preferred_element_type=jnp.float32)
        for d in range(peers):
            rows = y[MAIN * d : MAIN * (d + 1)]
            out_s[d, :, b * cut : (b + 1) * cut] = rows.astype(jnp.bfloat16)
            for t in range(rest):
                row = MAIN * peers + rest * d + t
                rest_s[d, cuts * t + b : cuts * t + b + 1, :] = y[row : row + 1]
        leave(b)
    for d in range(peers):
        out_s[d, :, size:] = rest_s[d].astype(jnp.bfloat16)
    leave(cuts)
    for copy in copies:
        copy.wait()


def project(keep, other, weights, peers, start, size):
    rows, _ = keep.shape
    width = packed_width(size, rows // peers)
    vmem = pl.BlockSpec(memory_space=pltpu.VMEM)
    return pl.pallas_call(
        functools.partial(project_kernel, start=start, size=size),
        in_specs=[vmem] * 3,
        out_specs=pl.BlockSpec(memory_space=pl.ANY),
        out_shape=pltpu.HBM((peers, MAIN, width), jnp.bfloat16),
        scratch_shapes=[
            pltpu.VMEM((peers, MAIN, width), jnp.bfloat16),
            pltpu.VMEM((peers, MAIN, width - size), jnp.float32),
            pltpu.SemaphoreType.DMA((width // (width - size),)),
        ],
        compiler_params=pltpu.CompilerParams(vmem_limit_bytes=VMEM_LIMIT),
        name=f"project_{start}",
    )(in_vmem(keep), in_vmem(other), in_vmem(weights))


def update_kernel(parts, residual, gate, out):
    total = parts[0].astype(jnp.float32)
    for d in range(1, parts.shape[0]):
        total = total + parts[d].astype(jnp.float32)
    out[...] = (residual[...] + gate[...] * total).astype(jnp.bfloat16)


def update(parts, residual, gate):
    vmem = pl.BlockSpec(memory_space=pltpu.VMEM)
    return pl.pallas_call(
        update_kernel,
        in_specs=[vmem] * 3,
        out_specs=vmem,
        out_shape=pltpu.VMEM(parts.shape[1:], jnp.bfloat16),
        compiler_params=pltpu.CompilerParams(vmem_limit_bytes=VMEM_LIMIT),
        name="update",
    )(in_vmem(parts), in_vmem(residual), in_vmem(gate))


def unpack_kernel(*refs, chunks):
    out = refs[-1]
    rest = out.shape[0] - MAIN
    cuts = MAIN // rest
    for packed, (start, size) in zip(refs, chunks):
        cut = size // cuts
        out[0:MAIN, start : start + size] = packed[:, :size]
        tail = packed[:, size:].astype(jnp.float32)
        for b in range(cuts):
            pieces = [tail[cuts * t + b : cuts * t + b + 1] for t in range(rest)]
            cols = slice(start + b * cut, start + (b + 1) * cut)
            out[MAIN:, cols] = jnp.concatenate(pieces, axis=0).astype(jnp.bfloat16)


def unpack(packed, rows, columns, chunks):
    vmem = pl.BlockSpec(memory_space=pltpu.VMEM)
    return pl.pallas_call(
        functools.partial(unpack_kernel, chunks=chunks),
        in_specs=[vmem] * len(packed),
        out_specs=vmem,
        out_shape=jax.ShapeDtypeStruct((rows, columns), jnp.bfloat16),
        compiler_params=pltpu.CompilerParams(vmem_limit_bytes=VMEM_LIMIT),
        name="unpack",
    )(*map(in_vmem, packed))


def shards(qkv, stale_kv, out_weight, residual, gate, patch_of_section):
    groups = lax.axis_size("head")
    sections = lax.axis_size("section")
    peers = groups // CORES
    tok = qkv.shape[1]
    columns = out_weight.shape[2]
    swap = [(i, i ^ 1) for i in range(groups)]
    same_core = [[CORES * k + c for k in range(peers)] for c in range(CORES)]
    chunks = []
    for parts in SPLIT:
        start = sum(size for _, size in chunks)
        chunks.append((start, columns * parts // sum(SPLIT)))

    core = lax.axis_index("head") % CORES
    scalars = jnp.stack([patch_of_section[0], core.astype(jnp.int32)])
    weight = out_weight[0]
    weight_other = lax.ppermute(weight, "head", swap)
    blocked = pack(qkv, groups)
    arrived = lax.all_to_all(blocked, "head", split_axis=0, concat_axis=0, tiled=True)
    kv = jnp.transpose(stale_kv[0], (1, 0, 2))

    keep, send, weights, _ = attend(scalars, arrived, prefetch(kv), kv, weight, weight_other)
    other = lax.ppermute(send, "head", swap)
    packed = stream(residual[0], gate, chunks)
    handed = []
    for i, (start, size) in enumerate(chunks):
        sums = project(keep, other, weights, peers, start, size)
        parts = lax.all_to_all(
            sums, "head", split_axis=0, concat_axis=0, tiled=True, axis_index_groups=same_core
        )
        updated = update(parts, packed[2 * i], packed[2 * i + 1])
        handed.append(
            lax.ppermute(updated, "section", [(j, (j + 1) % sections) for j in range(sections)])
        )
    return unpack(handed, tok, columns, chunks)[None]


def solution(mesh):
    placed = (
        P("section", "head", None, None),
        P("section", None, None, "head"),
        P("section", "head", None),
        P("section", "head", None),
        P("section", None),
        P("section"),
    )
    return jax.shard_map(
        shards, mesh=mesh, in_specs=placed, out_specs=P("section", "head", None), check_vma=False
    )
```

```python
import functools
import math

import jax
import jax.numpy as jnp
from jax import lax
from jax.experimental import pallas as pl
from jax.experimental.pallas import tpu as pltpu
from jax.sharding import PartitionSpec as P

HD = 128
CORES = 2
PAIR = 2
PLACES = ((0, 0), (0, 1), (2, 0), (2, 1), (1, 0), (1, 1), (3, 0), (3, 1))
MAIN = 16
SPLIT = (1, 1)
CHUNKS = 6
ATTEND_VMEM = 36 * 2**20
VMEM_LIMIT = 8 * 2**20


def in_vmem(x):
    return pltpu.with_memory_space_constraint(x, pltpu.VMEM)


def in_hbm(x):
    return pltpu.with_memory_space_constraint(x, pltpu.HBM)


def pack_kernel(qkv, out, in_s, rows_s, out_s, in_sems, out_sems, *, pieces):
    tok = qkv.shape[1]
    groups, _, width = out.shape
    part = tok // pieces
    step = groups // pieces_out(groups)
    arriving = []
    for n in range(pieces):
        rows = pl.ds(n * part, part)
        arriving.append(pltpu.make_async_copy(qkv.at[0, rows], in_s.at[rows], in_sems.at[n]))
        arriving[-1].start()
    for n in range(pieces):
        arriving[n].wait()
        for i in range(n * part, (n + 1) * part):
            value = in_s[i].astype(jnp.float32)
            for t in range(3):
                rows_s[t * tok + i : t * tok + i + 1, :] = value[t : t + 1]
    leaving = []
    for n in range(pieces_out(groups)):
        for g in range(n * step, (n + 1) * step):
            out_s[g] = rows_s[:, g * width : (g + 1) * width].astype(jnp.bfloat16)
        some = pl.ds(n * step, step)
        leaving.append(pltpu.make_async_copy(out_s.at[some], out.at[some], out_sems.at[n]))
        leaving[-1].start()
    for copy in leaving:
        copy.wait()


def pieces_out(groups):
    return 4 if groups % 4 == 0 else 1


def pack(qkv, groups):
    _, tok, _, columns = qkv.shape
    shape = (groups, 3 * tok, columns // groups)
    pieces = 3 if tok % 3 == 0 else 1
    anywhere = pl.BlockSpec(memory_space=pl.ANY)
    return pl.pallas_call(
        functools.partial(pack_kernel, pieces=pieces),
        in_specs=[anywhere],
        out_specs=anywhere,
        out_shape=pltpu.HBM(shape, jnp.bfloat16),
        scratch_shapes=[
            pltpu.VMEM((tok, 3, columns), jnp.bfloat16),
            pltpu.VMEM((3 * tok, columns), jnp.float32),
            pltpu.VMEM(shape, jnp.bfloat16),
            pltpu.SemaphoreType.DMA((pieces,)),
            pltpu.SemaphoreType.DMA((pieces_out(groups),)),
        ],
        compiler_params=pltpu.CompilerParams(vmem_limit_bytes=VMEM_LIMIT),
        name="pack",
    )(in_hbm(qkv))


def stream_kernel(residual, gate, *packed, chunks):
    rest = residual.shape[0] - MAIN
    cuts = MAIN // rest
    stream = residual[...].astype(jnp.float32)
    gates = gate[...]
    for i, (start, size) in enumerate(chunks):
        res_out, gate_out = packed[2 * i : 2 * i + 2]
        cut = size // cuts
        res_out[:, :size] = stream[:MAIN, start : start + size]
        gate_out[:, :size] = jnp.broadcast_to(gates[:, start : start + size], (MAIN, size))
        for b in range(cuts):
            cols = slice(start + b * cut, start + (b + 1) * cut)
            for t in range(rest):
                row = cuts * t + b
                res_out[row : row + 1, size:] = stream[MAIN + t : MAIN + t + 1, cols]
                gate_out[row : row + 1, size:] = gates[:, cols]


def stream(residual, gate, chunks):
    vmem = pl.BlockSpec(memory_space=pltpu.VMEM)
    packed = []
    for _, size in chunks:
        packed += [pltpu.VMEM((MAIN, packed_width(size, residual.shape[0])), jnp.float32)] * 2
    return pl.pallas_call(
        functools.partial(stream_kernel, chunks=chunks),
        in_specs=[vmem, vmem],
        out_specs=[vmem] * len(packed),
        out_shape=packed,
        compiler_params=pltpu.CompilerParams(vmem_limit_bytes=VMEM_LIMIT),
        name="stream",
    )(residual, gate)


def prefetch_kernel(kv, out, sems):
    copies = []
    for t in range(2):
        copies.append(pltpu.make_async_copy(kv.at[t, :, pl.ds(0, HD)], out.at[t], sems.at[t]))
        copies[-1].start()
    for copy in copies:
        copy.wait()


def prefetch(kv):
    return pl.pallas_call(
        prefetch_kernel,
        in_specs=[pl.BlockSpec(memory_space=pl.ANY)],
        out_specs=pl.BlockSpec(memory_space=pltpu.VMEM),
        out_shape=pltpu.VMEM((2, kv.shape[1], HD), kv.dtype),
        scratch_shapes=[pltpu.SemaphoreType.DMA((2,))],
        compiler_params=pltpu.CompilerParams(vmem_limit_bytes=2**20),
        name="prefetch",
    )(in_hbm(kv))


def attend_kernel(
    scalars, arrived, first_in, kv, w_keep, w_other,
    keep, send, w_out, first, q_s, fresh_s, sems, *kv_s, heads, chunk
):
    copies = []
    kv_s = (first.at[0], first.at[1]) + kv_s
    for h in range(1, heads):
        for t in range(2):
            n = 2 * (h - 1) + t
            copies.append(
                pltpu.make_async_copy(kv.at[t, :, pl.ds(h * HD, HD)], kv_s[2 * h + t], sems.at[n])
            )
    for i, w in enumerate((w_keep, w_other)):
        copies.append(pltpu.make_async_copy(w, w_out.at[i], sems.at[2 * heads - 2 + i]))
    for copy in copies:
        copy.start()
    groups = arrived.shape[0]
    tok = arrived.shape[1] // 3
    half = tok * groups // CORES
    peers = groups // CORES
    patch = tok * groups
    rest = tok - MAIN
    scale = math.log2(math.e) / math.sqrt(HD)
    core = lax.rem(scalars[1], CORES)
    here = lax.div(scalars[1], CORES)
    y_here, z_here = lax.div(here, PAIR), lax.rem(here, PAIR)
    for side in range(CORES):
        which = core if side == 0 else 1 - core
        for k, (dy, dz) in enumerate(PLACES):
            chip = lax.rem(y_here + dy, peers // PAIR) * PAIR + lax.rem(z_here + dz, PAIR)
            block = arrived[CORES * chip + which]
            for t in range(3):
                target = q_s if t == 0 else fresh_s.at[t - 1]
                rows = block[t * tok : (t + 1) * tok]
                target[pl.ds(side * half + MAIN * k, MAIN), :] = rows[:MAIN]
                target[pl.ds(side * half + MAIN * peers + rest * k, rest), :] = rows[MAIN:]
    own = pl.ds(pl.multiple_of(scalars[0] * patch, MAIN), patch)

    def ready(h, t):
        if h > 0:
            copies[2 * (h - 1) + t].wait()
        kv_s[2 * h + t][own, :] = fresh_s[t, :, h * HD : (h + 1) * HD]

    keys = kv_s[0].shape[0]
    for h in range(heads):
        ready(h, 0)
        ready(h, 1)
        cols = slice(h * HD, (h + 1) * HD)
        q = q_s[:, cols]

        def score(j):
            k = kv_s[2 * h][j * chunk : (j + 1) * chunk, :]
            return lax.dot_general(
                q, k, (((1,), (1,)), ((), ())), preferred_element_type=jnp.float32
            )

        top = total = acc = None
        upcoming = score(0)
        for j in range(keys // chunk):
            s = upcoming
            if j + 1 < keys // chunk:
                upcoming = score(j + 1)
            high = jnp.max(s, axis=1, keepdims=True)
            new_top = high if j == 0 else jnp.maximum(top, high)
            p = jnp.exp2((s - new_top) * scale)
            v = kv_s[2 * h + 1][j * chunk : (j + 1) * chunk, :]
            v = jnp.concatenate([v, jnp.ones_like(v)], axis=1)
            out = jnp.dot(p.astype(jnp.bfloat16), v, preferred_element_type=jnp.float32)
            out, part = out[:, :HD], out[:, HD:]
            if j == 0:
                total, acc = part, out
            else:
                fade = jnp.exp2((top - new_top) * scale)
                total = total * fade + part
                acc = acc * fade + out
            top = new_top
        done = (acc / total).astype(jnp.bfloat16)
        keep[:, cols] = done[:half]
        send[:, cols] = done[half:]
    for copy in copies[2 * heads - 2 :]:
        copy.wait()


def attend(scalars, arrived, first, kv, w_keep, w_other):
    groups, rows, width = arrived.shape
    keys = kv.shape[1]
    heads = width // HD
    patch = rows // 3 * groups
    result = pltpu.VMEM((patch // CORES, width), jnp.bfloat16)
    vmem = pl.BlockSpec(memory_space=pltpu.VMEM)
    anywhere = pl.BlockSpec(memory_space=pl.ANY)
    return pl.pallas_call(
        functools.partial(attend_kernel, heads=heads, chunk=keys // CHUNKS),
        in_specs=[pl.BlockSpec(memory_space=pltpu.SMEM), vmem, vmem] + [anywhere] * 3,
        out_specs=[vmem] * 4,
        out_shape=[
            result,
            result,
            pltpu.VMEM((CORES,) + w_keep.shape, w_keep.dtype),
            pltpu.VMEM(first.shape, first.dtype),
        ],
        scratch_shapes=[
            pltpu.VMEM((patch, width), jnp.bfloat16),
            pltpu.VMEM((2, patch, width), jnp.bfloat16),
            pltpu.SemaphoreType.DMA((2 * heads,)),
        ]
        + [pltpu.VMEM((keys, HD), jnp.bfloat16)] * (2 * heads - 2),
        input_output_aliases={2: 3},
        compiler_params=pltpu.CompilerParams(vmem_limit_bytes=ATTEND_VMEM),
        name="attend",
    )(scalars, in_vmem(arrived), in_vmem(first), *map(in_hbm, (kv, w_keep, w_other)))


def packed_width(size, tok):
    return size * tok // MAIN


def project_kernel(keep, other, weights, stay, across, ahead, behind, rest_s, *, start, size):
    blocks = [ref.at[n] for ref in (stay, across, ahead, behind) for n in range(ref.shape[0])]
    peers = len(blocks)
    cut = stay.shape[2] - size
    cuts = size // cut
    rest = MAIN // cuts
    both = jnp.concatenate([keep[...], other[...]], axis=1)
    for b in range(cuts):
        cols = slice(start + b * cut, start + (b + 1) * cut)
        w = jnp.concatenate([weights[i, :, cols] for i in range(CORES)], axis=0)
        y = jnp.dot(both, w, preferred_element_type=jnp.float32)
        for d in range(peers):
            rows = y[MAIN * d : MAIN * (d + 1)]
            blocks[d][:, b * cut : (b + 1) * cut] = rows.astype(jnp.bfloat16)
            for t in range(rest):
                row = MAIN * peers + rest * d + t
                rest_s[d, cuts * t + b : cuts * t + b + 1, :] = y[row : row + 1]
    for d in range(peers):
        blocks[d][:, size:] = rest_s[d].astype(jnp.bfloat16)


def project(keep, other, weights, peers, start, size):
    rows, _ = keep.shape
    width = packed_width(size, rows // peers)
    vmem = pl.BlockSpec(memory_space=pltpu.VMEM)
    return pl.pallas_call(
        functools.partial(project_kernel, start=start, size=size),
        in_specs=[vmem] * 3,
        out_specs=[vmem] * 4,
        out_shape=[pltpu.VMEM((n, MAIN, width), jnp.bfloat16) for n in (3, 1, 2, 2)],
        scratch_shapes=[pltpu.VMEM((peers, MAIN, width - size), jnp.float32)],
        compiler_params=pltpu.CompilerParams(vmem_limit_bytes=VMEM_LIMIT),
        name=f"project_{start}",
    )(in_vmem(keep), in_vmem(other), in_vmem(weights))


def add_kernel(*refs, picks):
    total = None
    for ref, pick in zip(refs, picks):
        term = ref[pick].astype(jnp.float32)
        total = term if total is None else total + term
    refs[-1][...] = total.astype(jnp.bfloat16)


def add(arrays, picks, name):
    vmem = pl.BlockSpec(memory_space=pltpu.VMEM)
    return pl.pallas_call(
        functools.partial(add_kernel, picks=picks),
        in_specs=[vmem] * len(arrays),
        out_specs=vmem,
        out_shape=pltpu.VMEM(arrays[0].shape[1:], jnp.bfloat16),
        compiler_params=pltpu.CompilerParams(vmem_limit_bytes=VMEM_LIMIT),
        name=name,
    )(*map(in_vmem, arrays))


def update_kernel(*refs):
    residual, gate, out = refs[-3:]
    total = refs[0][0].astype(jnp.float32)
    for ref in refs[1:-3]:
        total = total + ref[0].astype(jnp.float32)
    out[...] = (residual[...] + gate[...] * total).astype(jnp.bfloat16)


def update(arrays, residual, gate, name):
    vmem = pl.BlockSpec(memory_space=pltpu.VMEM)
    return pl.pallas_call(
        update_kernel,
        in_specs=[vmem] * (len(arrays) + 2),
        out_specs=vmem,
        out_shape=pltpu.VMEM(residual.shape, jnp.bfloat16),
        compiler_params=pltpu.CompilerParams(vmem_limit_bytes=VMEM_LIMIT),
        name=name,
    )(*map(in_vmem, (*arrays, residual, gate)))


def unpack_kernel(*refs, chunks):
    out = refs[-1]
    rest = out.shape[0] - MAIN
    cuts = MAIN // rest
    for packed, (start, size) in zip(refs, chunks):
        cut = size // cuts
        out[0:MAIN, start : start + size] = packed[:, :size]
        tail = packed[:, size:].astype(jnp.float32)
        for b in range(cuts):
            pieces = [tail[cuts * t + b : cuts * t + b + 1] for t in range(rest)]
            cols = slice(start + b * cut, start + (b + 1) * cut)
            out[MAIN:, cols] = jnp.concatenate(pieces, axis=0).astype(jnp.bfloat16)


def unpack(packed, rows, columns, chunks):
    vmem = pl.BlockSpec(memory_space=pltpu.VMEM)
    return pl.pallas_call(
        functools.partial(unpack_kernel, chunks=chunks),
        in_specs=[vmem] * len(packed),
        out_specs=vmem,
        out_shape=jax.ShapeDtypeStruct((rows, columns), jnp.bfloat16),
        compiler_params=pltpu.CompilerParams(vmem_limit_bytes=VMEM_LIMIT),
        name="unpack",
    )(*map(in_vmem, packed))


def shards(qkv, stale_kv, out_weight, residual, gate, patch_of_section):
    groups = lax.axis_size("head")
    sections = lax.axis_size("section")
    peers = groups // CORES
    tok = qkv.shape[1]
    columns = out_weight.shape[2]
    swap = [(i, i ^ 1) for i in range(groups)]
    chunks = []
    for parts in SPLIT:
        start = sum(size for _, size in chunks)
        chunks.append((start, columns * parts // sum(SPLIT)))

    scalars = jnp.stack([patch_of_section[0], lax.axis_index("head").astype(jnp.int32)])
    weight = out_weight[0]
    weight_other = lax.ppermute(weight, "head", swap)
    blocked = pack(qkv, groups)
    arrived = lax.all_to_all(blocked, "head", split_axis=0, concat_axis=0, tiled=True)
    kv = jnp.transpose(stale_kv[0], (1, 0, 2))

    keep, send, weights, _ = attend(scalars, arrived, prefetch(kv), kv, weight, weight_other)
    other = lax.ppermute(send, "head", swap)
    packed = stream(residual[0], gate, chunks)
    forward = [(j, (j + 1) % sections) for j in range(sections)]

    def along(x, dy, dz):
        route = [(i, (i + dy * PAIR * CORES) % groups ^ dz * CORES) for i in range(groups)]
        return lax.ppermute(x, "head", route)

    handed = []
    for i, (start, size) in enumerate(chunks):
        stay, across, ahead, behind = project(keep, other, weights, peers, start, size)
        from_z = along(across, 0, 1)
        from_last = along(ahead, 1, 0)
        from_next = along(behind, -1, 0)
        opposite = add((stay, from_z), (2, 0), f"opposite_{i}")
        from_opposite = along(opposite[None], 2, 0)
        pair = add((stay, from_last, from_next), (1, 1, 1), f"pair_{i}")
        from_pair = along(pair[None], 0, 1)
        terms = (stay, from_last, from_next, from_opposite, from_pair)
        updated = update(terms, packed[2 * i], packed[2 * i + 1], f"update_{i}")
        handed.append(lax.ppermute(updated, "section", forward))
    return unpack(handed, tok, columns, chunks)[None]


def solution(mesh):
    placed = (
        P("section", "head", None, None),
        P("section", None, None, "head"),
        P("section", "head", None),
        P("section", "head", None),
        P("section", None),
        P("section"),
    )
    return jax.shard_map(
        shards, mesh=mesh, in_specs=placed, out_specs=P("section", "head", None), check_vma=False
    )
```

```python
import functools
import math

import jax
import jax.numpy as jnp
from jax import lax
from jax.experimental import pallas as pl
from jax.experimental.pallas import tpu as pltpu
from jax.sharding import PartitionSpec as P

HD = 128
CORES = 2
PAIR = 2
PLACES = ((0, 0), (0, 1), (2, 0), (2, 1), (1, 0), (1, 1), (3, 0), (3, 1))
MAIN = 16
SPLIT = (1, 1)
CHUNKS = 6
ATTEND_VMEM = 36 * 2**20
VMEM_LIMIT = 8 * 2**20


def in_vmem(x):
    return pltpu.with_memory_space_constraint(x, pltpu.VMEM)


def in_hbm(x):
    return pltpu.with_memory_space_constraint(x, pltpu.HBM)


def pack_kernel(qkv, out, in_s, rows_s, out_s, in_sems, out_sems, *, pieces):
    tok = qkv.shape[1]
    groups, _, width = out.shape
    part = tok // pieces
    step = groups // pieces_out(groups)
    arriving = []
    for n in range(pieces):
        rows = pl.ds(n * part, part)
        arriving.append(pltpu.make_async_copy(qkv.at[0, rows], in_s.at[rows], in_sems.at[n]))
        arriving[-1].start()
    for n in range(pieces):
        arriving[n].wait()
        for i in range(n * part, (n + 1) * part):
            value = in_s[i].astype(jnp.float32)
            for t in range(3):
                rows_s[t * tok + i : t * tok + i + 1, :] = value[t : t + 1]
    leaving = []
    for n in range(pieces_out(groups)):
        for g in range(n * step, (n + 1) * step):
            out_s[g] = rows_s[:, g * width : (g + 1) * width].astype(jnp.bfloat16)
        some = pl.ds(n * step, step)
        leaving.append(pltpu.make_async_copy(out_s.at[some], out.at[some], out_sems.at[n]))
        leaving[-1].start()
    for copy in leaving:
        copy.wait()


def pieces_out(groups):
    return 4 if groups % 4 == 0 else 1


def pack(qkv, groups):
    _, tok, _, columns = qkv.shape
    shape = (groups, 3 * tok, columns // groups)
    pieces = 3 if tok % 3 == 0 else 1
    anywhere = pl.BlockSpec(memory_space=pl.ANY)
    return pl.pallas_call(
        functools.partial(pack_kernel, pieces=pieces),
        in_specs=[anywhere],
        out_specs=anywhere,
        out_shape=pltpu.HBM(shape, jnp.bfloat16),
        scratch_shapes=[
            pltpu.VMEM((tok, 3, columns), jnp.bfloat16),
            pltpu.VMEM((3 * tok, columns), jnp.float32),
            pltpu.VMEM(shape, jnp.bfloat16),
            pltpu.SemaphoreType.DMA((pieces,)),
            pltpu.SemaphoreType.DMA((pieces_out(groups),)),
        ],
        compiler_params=pltpu.CompilerParams(vmem_limit_bytes=VMEM_LIMIT),
        name="pack",
    )(in_hbm(qkv))


def stream_kernel(residual, gate, *packed, chunks):
    rest = residual.shape[0] - MAIN
    cuts = MAIN // rest
    stream = residual[...].astype(jnp.float32)
    gates = gate[...]
    for i, (start, size) in enumerate(chunks):
        res_out, gate_out = packed[2 * i : 2 * i + 2]
        cut = size // cuts
        res_out[:, :size] = stream[:MAIN, start : start + size]
        gate_out[:, :size] = jnp.broadcast_to(gates[:, start : start + size], (MAIN, size))
        for b in range(cuts):
            cols = slice(start + b * cut, start + (b + 1) * cut)
            for t in range(rest):
                row = cuts * t + b
                res_out[row : row + 1, size:] = stream[MAIN + t : MAIN + t + 1, cols]
                gate_out[row : row + 1, size:] = gates[:, cols]


def stream(residual, gate, chunks):
    vmem = pl.BlockSpec(memory_space=pltpu.VMEM)
    packed = []
    for _, size in chunks:
        packed += [pltpu.VMEM((MAIN, packed_width(size, residual.shape[0])), jnp.float32)] * 2
    return pl.pallas_call(
        functools.partial(stream_kernel, chunks=chunks),
        in_specs=[vmem, vmem],
        out_specs=[vmem] * len(packed),
        out_shape=packed,
        compiler_params=pltpu.CompilerParams(vmem_limit_bytes=VMEM_LIMIT),
        name="stream",
    )(residual, gate)


def prefetch_kernel(kv, out, sems):
    copies = []
    for t in range(2):
        copies.append(pltpu.make_async_copy(kv.at[t, :, pl.ds(0, HD)], out.at[t], sems.at[t]))
        copies[-1].start()
    for copy in copies:
        copy.wait()


def prefetch(kv):
    return pl.pallas_call(
        prefetch_kernel,
        in_specs=[pl.BlockSpec(memory_space=pl.ANY)],
        out_specs=pl.BlockSpec(memory_space=pltpu.VMEM),
        out_shape=pltpu.VMEM((2, kv.shape[1], HD), kv.dtype),
        scratch_shapes=[pltpu.SemaphoreType.DMA((2,))],
        compiler_params=pltpu.CompilerParams(vmem_limit_bytes=2**20),
        name="prefetch",
    )(in_hbm(kv))


def attend_kernel(
    scalars, arrived, first_in, kv, w_keep, w_other,
    keep, send, w_out, first, q_s, fresh_s, sems, *kv_s, heads, chunk
):
    copies = []
    kv_s = (first.at[0], first.at[1]) + kv_s
    for h in range(1, heads):
        for t in range(2):
            n = 2 * (h - 1) + t
            copies.append(
                pltpu.make_async_copy(kv.at[t, :, pl.ds(h * HD, HD)], kv_s[2 * h + t], sems.at[n])
            )
    for i, w in enumerate((w_keep, w_other)):
        copies.append(pltpu.make_async_copy(w, w_out.at[i], sems.at[2 * heads - 2 + i]))
    for copy in copies:
        copy.start()
    groups = arrived.shape[0]
    tok = arrived.shape[1] // 3
    half = tok * groups // CORES
    peers = groups // CORES
    patch = tok * groups
    rest = tok - MAIN
    scale = math.log2(math.e) / math.sqrt(HD)
    core = lax.rem(scalars[1], CORES)
    here = lax.div(scalars[1], CORES)
    y_here, z_here = lax.div(here, PAIR), lax.rem(here, PAIR)
    for side in range(CORES):
        which = core if side == 0 else 1 - core
        for k, (dy, dz) in enumerate(PLACES):
            chip = lax.rem(y_here + dy, peers // PAIR) * PAIR + lax.rem(z_here + dz, PAIR)
            block = arrived[CORES * chip + which]
            for t in range(3):
                target = q_s if t == 0 else fresh_s.at[t - 1]
                rows = block[t * tok : (t + 1) * tok]
                target[pl.ds(side * half + MAIN * k, MAIN), :] = rows[:MAIN]
                target[pl.ds(side * half + MAIN * peers + rest * k, rest), :] = rows[MAIN:]
    own = pl.ds(pl.multiple_of(scalars[0] * patch, MAIN), patch)

    def ready(h, t):
        if h > 0:
            copies[2 * (h - 1) + t].wait()
        kv_s[2 * h + t][own, :] = fresh_s[t, :, h * HD : (h + 1) * HD]

    keys = kv_s[0].shape[0]
    for h in range(heads):
        ready(h, 0)
        ready(h, 1)
        cols = slice(h * HD, (h + 1) * HD)
        q = q_s[:, cols]

        def score(j):
            k = kv_s[2 * h][j * chunk : (j + 1) * chunk, :]
            return lax.dot_general(
                q, k, (((1,), (1,)), ((), ())), preferred_element_type=jnp.float32
            )

        top = total = acc = None
        upcoming = score(0)
        for j in range(keys // chunk):
            s = upcoming
            if j + 1 < keys // chunk:
                upcoming = score(j + 1)
            high = jnp.max(s, axis=1, keepdims=True)
            new_top = high if j == 0 else jnp.maximum(top, high)
            p = jnp.exp2((s - new_top) * scale)
            v = kv_s[2 * h + 1][j * chunk : (j + 1) * chunk, :]
            v = jnp.concatenate([v, jnp.ones_like(v)], axis=1)
            out = jnp.dot(p.astype(jnp.bfloat16), v, preferred_element_type=jnp.float32)
            out, part = out[:, :HD], out[:, HD:]
            if j == 0:
                total, acc = part, out
            else:
                fade = jnp.exp2((top - new_top) * scale)
                total = total * fade + part
                acc = acc * fade + out
            top = new_top
        done = (acc / total).astype(jnp.bfloat16)
        keep[:, cols] = done[:half]
        send[:, cols] = done[half:]
    for copy in copies[2 * heads - 2 :]:
        copy.wait()


def attend(scalars, arrived, first, kv, w_keep, w_other):
    groups, rows, width = arrived.shape
    keys = kv.shape[1]
    heads = width // HD
    patch = rows // 3 * groups
    result = pltpu.VMEM((patch // CORES, width), jnp.bfloat16)
    vmem = pl.BlockSpec(memory_space=pltpu.VMEM)
    anywhere = pl.BlockSpec(memory_space=pl.ANY)
    return pl.pallas_call(
        functools.partial(attend_kernel, heads=heads, chunk=keys // CHUNKS),
        in_specs=[pl.BlockSpec(memory_space=pltpu.SMEM), vmem, vmem] + [anywhere] * 3,
        out_specs=[vmem] * 4,
        out_shape=[
            result,
            result,
            pltpu.VMEM((CORES,) + w_keep.shape, w_keep.dtype),
            pltpu.VMEM(first.shape, first.dtype),
        ],
        scratch_shapes=[
            pltpu.VMEM((patch, width), jnp.bfloat16),
            pltpu.VMEM((2, patch, width), jnp.bfloat16),
            pltpu.SemaphoreType.DMA((2 * heads,)),
        ]
        + [pltpu.VMEM((keys, HD), jnp.bfloat16)] * (2 * heads - 2),
        input_output_aliases={2: 3},
        compiler_params=pltpu.CompilerParams(vmem_limit_bytes=ATTEND_VMEM),
        name="attend",
    )(scalars, in_vmem(arrived), in_vmem(first), *map(in_hbm, (kv, w_keep, w_other)))


def packed_width(size, tok):
    return size * tok // MAIN


def project_kernel(keep, other, weights, after, stay, across, ahead, behind, rest_s, *, start, size):
    blocks = [ref.at[n] for ref in (stay, across, ahead, behind) for n in range(ref.shape[0])]
    peers = len(blocks)
    cut = stay.shape[2] - size
    cuts = size // cut
    rest = MAIN // cuts
    both = jnp.concatenate([keep[...], other[...]], axis=1)
    for b in range(cuts):
        cols = slice(start + b * cut, start + (b + 1) * cut)
        w = jnp.concatenate([weights[i, :, cols] for i in range(CORES)], axis=0)
        y = jnp.dot(both, w, preferred_element_type=jnp.float32)
        for d in range(peers):
            rows = y[MAIN * d : MAIN * (d + 1)]
            blocks[d][:, b * cut : (b + 1) * cut] = rows.astype(jnp.bfloat16)
            for t in range(rest):
                row = MAIN * peers + rest * d + t
                rest_s[d, cuts * t + b : cuts * t + b + 1, :] = y[row : row + 1]
    for d in range(peers):
        blocks[d][:, size:] = rest_s[d].astype(jnp.bfloat16)


def project(keep, other, weights, after, peers, start, size):
    rows, _ = keep.shape
    width = packed_width(size, rows // peers)
    vmem = pl.BlockSpec(memory_space=pltpu.VMEM)
    return pl.pallas_call(
        functools.partial(project_kernel, start=start, size=size),
        in_specs=[vmem] * 3 + [pl.BlockSpec(memory_space=pl.ANY)],
        out_specs=[vmem] * 4,
        out_shape=[pltpu.VMEM((n, MAIN, width), jnp.bfloat16) for n in (3, 1, 2, 2)],
        scratch_shapes=[pltpu.VMEM((peers, MAIN, width - size), jnp.float32)],
        compiler_params=pltpu.CompilerParams(vmem_limit_bytes=VMEM_LIMIT),
        name=f"project_{start}",
    )(in_vmem(keep), in_vmem(other), in_vmem(weights), after)


def add_kernel(*refs, picks):
    total = None
    for ref, pick in zip(refs, picks):
        term = ref[pick].astype(jnp.float32)
        total = term if total is None else total + term
    refs[-1][...] = total.astype(jnp.bfloat16)


def add(arrays, after, picks, name):
    vmem = pl.BlockSpec(memory_space=pltpu.VMEM)
    return pl.pallas_call(
        functools.partial(add_kernel, picks=picks),
        in_specs=[vmem] * len(arrays) + [pl.BlockSpec(memory_space=pl.ANY)],
        out_specs=vmem,
        out_shape=pltpu.VMEM(arrays[0].shape[1:], jnp.bfloat16),
        compiler_params=pltpu.CompilerParams(vmem_limit_bytes=VMEM_LIMIT),
        name=name,
    )(*map(in_vmem, arrays), after)


def update_kernel(*refs):
    residual, gate, out = refs[-3:]
    total = refs[0][0].astype(jnp.float32)
    for ref in refs[1:-3]:
        total = total + ref[0].astype(jnp.float32)
    out[...] = (residual[...] + gate[...] * total).astype(jnp.bfloat16)


def update(arrays, residual, gate, name):
    vmem = pl.BlockSpec(memory_space=pltpu.VMEM)
    return pl.pallas_call(
        update_kernel,
        in_specs=[vmem] * (len(arrays) + 2),
        out_specs=vmem,
        out_shape=pltpu.VMEM(residual.shape, jnp.bfloat16),
        compiler_params=pltpu.CompilerParams(vmem_limit_bytes=VMEM_LIMIT),
        name=name,
    )(*map(in_vmem, (*arrays, residual, gate)))


def unpack_kernel(*refs, chunks):
    out = refs[-1]
    rest = out.shape[0] - MAIN
    cuts = MAIN // rest
    for packed, (start, size) in zip(refs, chunks):
        cut = size // cuts
        out[0:MAIN, start : start + size] = packed[:, :size]
        tail = packed[:, size:].astype(jnp.float32)
        for b in range(cuts):
            pieces = [tail[cuts * t + b : cuts * t + b + 1] for t in range(rest)]
            cols = slice(start + b * cut, start + (b + 1) * cut)
            out[MAIN:, cols] = jnp.concatenate(pieces, axis=0).astype(jnp.bfloat16)


def unpack(packed, rows, columns, chunks):
    vmem = pl.BlockSpec(memory_space=pltpu.VMEM)
    return pl.pallas_call(
        functools.partial(unpack_kernel, chunks=chunks),
        in_specs=[vmem] * len(packed),
        out_specs=vmem,
        out_shape=jax.ShapeDtypeStruct((rows, columns), jnp.bfloat16),
        compiler_params=pltpu.CompilerParams(vmem_limit_bytes=VMEM_LIMIT),
        name="unpack",
    )(*map(in_vmem, packed))


def shards(qkv, stale_kv, out_weight, residual, gate, patch_of_section):
    groups = lax.axis_size("head")
    sections = lax.axis_size("section")
    peers = groups // CORES
    tok = qkv.shape[1]
    columns = out_weight.shape[2]
    swap = [(i, i ^ 1) for i in range(groups)]
    chunks = []
    for parts in SPLIT:
        start = sum(size for _, size in chunks)
        chunks.append((start, columns * parts // sum(SPLIT)))

    scalars = jnp.stack([patch_of_section[0], lax.axis_index("head").astype(jnp.int32)])
    weight = out_weight[0]
    weight_other = lax.ppermute(weight, "head", swap)
    blocked = pack(qkv, groups)
    arrived = lax.all_to_all(blocked, "head", split_axis=0, concat_axis=0, tiled=True)
    kv = jnp.transpose(stale_kv[0], (1, 0, 2))

    keep, send, weights, _ = attend(scalars, arrived, prefetch(kv), kv, weight, weight_other)
    other = lax.ppermute(send, "head", swap)
    packed = stream(residual[0], gate, chunks)
    forward = [(j, (j + 1) % sections) for j in range(sections)]

    def along(x, dy, dz):
        route = [(i, (i + dy * PAIR * CORES) % groups ^ dz * CORES) for i in range(groups)]
        return lax.ppermute(x, "head", route)

    handed = []
    turns = [keep] * 3
    for i, (start, size) in enumerate(chunks):
        stay, across, ahead, behind = project(keep, other, weights, turns[0], peers, start, size)
        from_z = along(across, 0, 1)
        from_last = along(ahead, 1, 0)
        from_next = along(behind, -1, 0)
        opposite = add((stay, from_z), turns[1], (2, 0), f"opposite_{i}")
        from_opposite = along(opposite[None], 2, 0)
        pair = add((stay, from_last, from_next), turns[2], (1, 1, 1), f"pair_{i}")
        from_pair = along(pair[None], 0, 1)
        terms = (stay, from_last, from_next, from_opposite, from_pair)
        updated = update(terms, packed[2 * i], packed[2 * i + 1], f"update_{i}")
        handed.append(lax.ppermute(updated, "section", forward))
        turns = [across, pair, updated]
    return unpack(handed, tok, columns, chunks)[None]


def solution(mesh):
    placed = (
        P("section", "head", None, None),
        P("section", None, None, "head"),
        P("section", "head", None),
        P("section", "head", None),
        P("section", None),
        P("section"),
    )
    return jax.shard_map(
        shards, mesh=mesh, in_specs=placed, out_specs=P("section", "head", None), check_vma=False
    )
```

```python
import functools
import math

import jax
import jax.numpy as jnp
from jax import lax
from jax.experimental import pallas as pl
from jax.experimental.pallas import tpu as pltpu
from jax.sharding import PartitionSpec as P

HD = 128
CORES = 2
PAIR = 2
PLACES = ((0, 0), (0, 1), (1, 1), (3, 1), (1, 0), (3, 0), (2, 0), (2, 1))
MAIN = 16
SPLIT = (1, 2)
CHUNKS = 6
ATTEND_VMEM = 36 * 2**20
VMEM_LIMIT = 8 * 2**20


def in_vmem(x):
    return pltpu.with_memory_space_constraint(x, pltpu.VMEM)


def in_hbm(x):
    return pltpu.with_memory_space_constraint(x, pltpu.HBM)


def pack_kernel(qkv, out, in_s, rows_s, out_s, in_sems, out_sems, *, pieces):
    tok = qkv.shape[1]
    groups, _, width = out.shape
    part = tok // pieces
    step = groups // pieces_out(groups)
    arriving = []
    for n in range(pieces):
        rows = pl.ds(n * part, part)
        arriving.append(pltpu.make_async_copy(qkv.at[0, rows], in_s.at[rows], in_sems.at[n]))
        arriving[-1].start()
    for n in range(pieces):
        arriving[n].wait()
        for i in range(n * part, (n + 1) * part):
            value = in_s[i].astype(jnp.float32)
            for t in range(3):
                rows_s[t * tok + i : t * tok + i + 1, :] = value[t : t + 1]
    leaving = []
    for n in range(pieces_out(groups)):
        for g in range(n * step, (n + 1) * step):
            out_s[g] = rows_s[:, g * width : (g + 1) * width].astype(jnp.bfloat16)
        some = pl.ds(n * step, step)
        leaving.append(pltpu.make_async_copy(out_s.at[some], out.at[some], out_sems.at[n]))
        leaving[-1].start()
    for copy in leaving:
        copy.wait()


def pieces_out(groups):
    return 4 if groups % 4 == 0 else 1


def pack(qkv, groups):
    _, tok, _, columns = qkv.shape
    shape = (groups, 3 * tok, columns // groups)
    pieces = 3 if tok % 3 == 0 else 1
    anywhere = pl.BlockSpec(memory_space=pl.ANY)
    return pl.pallas_call(
        functools.partial(pack_kernel, pieces=pieces),
        in_specs=[anywhere],
        out_specs=anywhere,
        out_shape=pltpu.HBM(shape, jnp.bfloat16),
        scratch_shapes=[
            pltpu.VMEM((tok, 3, columns), jnp.bfloat16),
            pltpu.VMEM((3 * tok, columns), jnp.float32),
            pltpu.VMEM(shape, jnp.bfloat16),
            pltpu.SemaphoreType.DMA((pieces,)),
            pltpu.SemaphoreType.DMA((pieces_out(groups),)),
        ],
        compiler_params=pltpu.CompilerParams(vmem_limit_bytes=VMEM_LIMIT),
        name="pack",
    )(in_hbm(qkv))


def stream_kernel(residual, gate, *packed, chunks):
    rest = residual.shape[0] - MAIN
    cuts = MAIN // rest
    stream = residual[...].astype(jnp.float32)
    gates = gate[...]
    for i, (start, size) in enumerate(chunks):
        res_out, gate_out = packed[2 * i : 2 * i + 2]
        cut = size // cuts
        res_out[:, :size] = stream[:MAIN, start : start + size]
        gate_out[:, :size] = jnp.broadcast_to(gates[:, start : start + size], (MAIN, size))
        for b in range(cuts):
            cols = slice(start + b * cut, start + (b + 1) * cut)
            for t in range(rest):
                row = cuts * t + b
                res_out[row : row + 1, size:] = stream[MAIN + t : MAIN + t + 1, cols]
                gate_out[row : row + 1, size:] = gates[:, cols]


def stream(residual, gate, chunks):
    vmem = pl.BlockSpec(memory_space=pltpu.VMEM)
    packed = []
    for _, size in chunks:
        packed += [pltpu.VMEM((MAIN, packed_width(size, residual.shape[0])), jnp.float32)] * 2
    return pl.pallas_call(
        functools.partial(stream_kernel, chunks=chunks),
        in_specs=[vmem, vmem],
        out_specs=[vmem] * len(packed),
        out_shape=packed,
        compiler_params=pltpu.CompilerParams(vmem_limit_bytes=VMEM_LIMIT),
        name="stream",
    )(residual, gate)


def prefetch_kernel(kv, out, sems):
    copies = []
    for t in range(2):
        copies.append(pltpu.make_async_copy(kv.at[t, :, pl.ds(0, HD)], out.at[t], sems.at[t]))
        copies[-1].start()
    for copy in copies:
        copy.wait()


def prefetch(kv):
    return pl.pallas_call(
        prefetch_kernel,
        in_specs=[pl.BlockSpec(memory_space=pl.ANY)],
        out_specs=pl.BlockSpec(memory_space=pltpu.VMEM),
        out_shape=pltpu.VMEM((2, kv.shape[1], HD), kv.dtype),
        scratch_shapes=[pltpu.SemaphoreType.DMA((2,))],
        compiler_params=pltpu.CompilerParams(vmem_limit_bytes=2**20),
        name="prefetch",
    )(in_hbm(kv))


def attend_kernel(
    scalars, arrived, first_in, kv, w_keep, w_other,
    keep, send, w_out, first, q_s, fresh_s, sems, *kv_s, heads, chunk
):
    copies = []
    kv_s = (first.at[0], first.at[1]) + kv_s
    for h in range(1, heads):
        for t in range(2):
            n = 2 * (h - 1) + t
            copies.append(
                pltpu.make_async_copy(kv.at[t, :, pl.ds(h * HD, HD)], kv_s[2 * h + t], sems.at[n])
            )
    for i, w in enumerate((w_keep, w_other)):
        copies.append(pltpu.make_async_copy(w, w_out.at[i], sems.at[2 * heads - 2 + i]))
    for copy in copies:
        copy.start()
    groups = arrived.shape[0]
    tok = arrived.shape[1] // 3
    half = tok * groups // CORES
    peers = groups // CORES
    patch = tok * groups
    rest = tok - MAIN
    scale = math.log2(math.e) / math.sqrt(HD)
    core = lax.rem(scalars[1], CORES)
    here = lax.div(scalars[1], CORES)
    y_here, z_here = lax.div(here, PAIR), lax.rem(here, PAIR)
    for side in range(CORES):
        which = core if side == 0 else 1 - core
        for k, (dy, dz) in enumerate(PLACES):
            chip = lax.rem(y_here + dy, peers // PAIR) * PAIR + lax.rem(z_here + dz, PAIR)
            block = arrived[CORES * chip + which]
            for t in range(3):
                target = q_s if t == 0 else fresh_s.at[t - 1]
                rows = block[t * tok : (t + 1) * tok]
                target[pl.ds(side * half + MAIN * k, MAIN), :] = rows[:MAIN]
                target[pl.ds(side * half + MAIN * peers + rest * k, rest), :] = rows[MAIN:]
    own = pl.ds(pl.multiple_of(scalars[0] * patch, MAIN), patch)

    def ready(h, t):
        if h > 0:
            copies[2 * (h - 1) + t].wait()
        kv_s[2 * h + t][own, :] = fresh_s[t, :, h * HD : (h + 1) * HD]

    keys = kv_s[0].shape[0]
    for h in range(heads):
        ready(h, 0)
        ready(h, 1)
        cols = slice(h * HD, (h + 1) * HD)
        q = q_s[:, cols]

        def score(j):
            k = kv_s[2 * h][j * chunk : (j + 1) * chunk, :]
            return lax.dot_general(
                q, k, (((1,), (1,)), ((), ())), preferred_element_type=jnp.float32
            )

        top = total = acc = None
        upcoming = score(0)
        for j in range(keys // chunk):
            s = upcoming
            if j + 1 < keys // chunk:
                upcoming = score(j + 1)
            high = jnp.max(s, axis=1, keepdims=True)
            new_top = high if j == 0 else jnp.maximum(top, high)
            p = jnp.exp2((s - new_top) * scale)
            v = kv_s[2 * h + 1][j * chunk : (j + 1) * chunk, :]
            v = jnp.concatenate([v, jnp.ones_like(v)], axis=1)
            out = jnp.dot(p.astype(jnp.bfloat16), v, preferred_element_type=jnp.float32)
            out, part = out[:, :HD], out[:, HD:]
            if j == 0:
                total, acc = part, out
            else:
                fade = jnp.exp2((top - new_top) * scale)
                total = total * fade + part
                acc = acc * fade + out
            top = new_top
        done = (acc / total).astype(jnp.bfloat16)
        keep[:, cols] = done[:half]
        send[:, cols] = done[half:]
    for copy in copies[2 * heads - 2 :]:
        copy.wait()


def attend(scalars, arrived, first, kv, w_keep, w_other):
    groups, rows, width = arrived.shape
    keys = kv.shape[1]
    heads = width // HD
    patch = rows // 3 * groups
    result = pltpu.VMEM((patch // CORES, width), jnp.bfloat16)
    vmem = pl.BlockSpec(memory_space=pltpu.VMEM)
    anywhere = pl.BlockSpec(memory_space=pl.ANY)
    return pl.pallas_call(
        functools.partial(attend_kernel, heads=heads, chunk=keys // CHUNKS),
        in_specs=[pl.BlockSpec(memory_space=pltpu.SMEM), vmem, vmem] + [anywhere] * 3,
        out_specs=[vmem] * 4,
        out_shape=[
            result,
            result,
            pltpu.VMEM((CORES,) + w_keep.shape, w_keep.dtype),
            pltpu.VMEM(first.shape, first.dtype),
        ],
        scratch_shapes=[
            pltpu.VMEM((patch, width), jnp.bfloat16),
            pltpu.VMEM((2, patch, width), jnp.bfloat16),
            pltpu.SemaphoreType.DMA((2 * heads,)),
        ]
        + [pltpu.VMEM((keys, HD), jnp.bfloat16)] * (2 * heads - 2),
        input_output_aliases={2: 3},
        compiler_params=pltpu.CompilerParams(vmem_limit_bytes=ATTEND_VMEM),
        name="attend",
    )(scalars, in_vmem(arrived), in_vmem(first), *map(in_hbm, (kv, w_keep, w_other)))


def packed_width(size, tok):
    return size * tok // MAIN


def project_kernel(keep, other, weights, *refs, chunks):
    outs, rest_s = refs[:-1], refs[-1]
    peers = rest_s.shape[0]
    rest = keep.shape[0] // peers - MAIN
    cuts = MAIN // rest
    both = jnp.concatenate([keep[...], other[...]], axis=1)
    offset = 0
    for i, (start, size) in enumerate(chunks):
        cut = size // cuts
        width = size + cut
        span = pl.ds(offset, width)
        blocks = [ref.at[n, :, span] for ref in outs for n in range(ref.shape[0])]
        for b in range(cuts):
            cols = slice(start + b * cut, start + (b + 1) * cut)
            w = jnp.concatenate([weights[n, :, cols] for n in range(CORES)], axis=0)
            y = jnp.dot(both, w, preferred_element_type=jnp.float32)
            for d in range(peers):
                rows = y[MAIN * d : MAIN * (d + 1)]
                blocks[d][:, b * cut : (b + 1) * cut] = rows.astype(jnp.bfloat16)
                for t in range(rest):
                    row = MAIN * peers + rest * d + t
                    rest_s[d, cuts * t + b : cuts * t + b + 1, :cut] = y[row : row + 1]
        for d in range(peers):
            blocks[d][:, size:] = rest_s[d, :, :cut].astype(jnp.bfloat16)
        offset += width


def project(keep, other, weights, peers, chunks):
    rows, _ = keep.shape
    widths = [packed_width(size, rows // peers) for _, size in chunks]
    vmem = pl.BlockSpec(memory_space=pltpu.VMEM)
    shapes = [(1, MAIN, sum(widths))] * peers
    deepest = max(width - size for width, (_, size) in zip(widths, chunks))
    return pl.pallas_call(
        functools.partial(project_kernel, chunks=chunks),
        in_specs=[vmem] * 3,
        out_specs=[vmem] * len(shapes),
        out_shape=[pltpu.VMEM(shape, jnp.bfloat16) for shape in shapes],
        scratch_shapes=[pltpu.VMEM((peers, MAIN, deepest), jnp.float32)],
        compiler_params=pltpu.CompilerParams(vmem_limit_bytes=VMEM_LIMIT),
        name="project",
    )(in_vmem(keep), in_vmem(other), in_vmem(weights))


def total_of(refs, picks, width):
    total = None
    for ref, (n, offset) in zip(refs, picks):
        term = ref[n, :, offset : offset + width].astype(jnp.float32)
        total = term if total is None else total + term
    return total


def add_kernel(*refs, picks):
    out = refs[-1]
    out[0] = total_of(refs, picks, out.shape[2]).astype(jnp.bfloat16)


def add(arrays, after, picks, width, name):
    vmem = pl.BlockSpec(memory_space=pltpu.VMEM)
    return pl.pallas_call(
        functools.partial(add_kernel, picks=picks),
        in_specs=[vmem] * len(arrays) + [pl.BlockSpec(memory_space=pl.ANY)],
        out_specs=vmem,
        out_shape=pltpu.VMEM((1, MAIN, width), jnp.bfloat16),
        compiler_params=pltpu.CompilerParams(vmem_limit_bytes=VMEM_LIMIT),
        name=name,
    )(*map(in_vmem, arrays), after)


def update_kernel(*refs, picks):
    residual, gate, out = refs[-3:]
    total = total_of(refs, picks, out.shape[1])
    out[...] = (residual[...] + gate[...] * total).astype(jnp.bfloat16)


def update(arrays, picks, residual, gate, name):
    vmem = pl.BlockSpec(memory_space=pltpu.VMEM)
    return pl.pallas_call(
        functools.partial(update_kernel, picks=picks),
        in_specs=[vmem] * (len(arrays) + 2),
        out_specs=vmem,
        out_shape=pltpu.VMEM(residual.shape, jnp.bfloat16),
        compiler_params=pltpu.CompilerParams(vmem_limit_bytes=VMEM_LIMIT),
        name=name,
    )(*map(in_vmem, (*arrays, residual, gate)))


def unpack_kernel(*refs, chunks):
    out = refs[-1]
    rest = out.shape[0] - MAIN
    cuts = MAIN // rest
    for packed, (start, size) in zip(refs, chunks):
        cut = size // cuts
        out[0:MAIN, start : start + size] = packed[:, :size]
        tail = packed[:, size:].astype(jnp.float32)
        for b in range(cuts):
            pieces = [tail[cuts * t + b : cuts * t + b + 1] for t in range(rest)]
            cols = slice(start + b * cut, start + (b + 1) * cut)
            out[MAIN:, cols] = jnp.concatenate(pieces, axis=0).astype(jnp.bfloat16)


def unpack(packed, rows, columns, chunks):
    vmem = pl.BlockSpec(memory_space=pltpu.VMEM)
    return pl.pallas_call(
        functools.partial(unpack_kernel, chunks=chunks),
        in_specs=[vmem] * len(packed),
        out_specs=vmem,
        out_shape=jax.ShapeDtypeStruct((rows, columns), jnp.bfloat16),
        compiler_params=pltpu.CompilerParams(vmem_limit_bytes=VMEM_LIMIT),
        name="unpack",
    )(*map(in_vmem, packed))


def shards(qkv, stale_kv, out_weight, residual, gate, patch_of_section):
    groups = lax.axis_size("head")
    sections = lax.axis_size("section")
    peers = groups // CORES
    tok = qkv.shape[1]
    columns = out_weight.shape[2]
    swap = [(i, i ^ 1) for i in range(groups)]
    chunks = []
    for parts in SPLIT:
        start = sum(size for _, size in chunks)
        chunks.append((start, columns * parts // sum(SPLIT)))

    scalars = jnp.stack([patch_of_section[0], lax.axis_index("head").astype(jnp.int32)])
    weight = out_weight[0]
    weight_other = lax.ppermute(weight, "head", swap)
    blocked = pack(qkv, groups)
    arrived = lax.all_to_all(blocked, "head", split_axis=0, concat_axis=0, tiled=True)
    kv = jnp.transpose(stale_kv[0], (1, 0, 2))

    keep, send, weights, _ = attend(scalars, arrived, prefetch(kv), kv, weight, weight_other)
    other = lax.ppermute(send, "head", swap)
    packed = stream(residual[0], gate, chunks)
    forward = [(j, (j + 1) % sections) for j in range(sections)]

    def along(x, dy, dz):
        route = [(i, (i + dy * PAIR * CORES) % groups ^ dz * CORES) for i in range(groups)]
        return lax.ppermute(x, "head", route)

    mine, pair, ahead_far, behind_far, ahead, behind, opposite, across = project(
        keep, other, weights, peers, chunks
    )
    far = (pair, along(ahead_far, 1, 0), along(behind_far, -1, 0))
    across = along(across, 0, 1)
    near = (mine, along(ahead, 1, 0), along(behind, -1, 0))
    handed = []
    turn = keep
    offset = 0
    width = mine.shape[2]
    sums = add(far, keep, ((0, 0),) * 3, width, "pair")
    from_pair = along(sums, 0, 1)
    sums = add((opposite, across), sums, ((0, 0),) * 2, width, "opposite")
    from_opposite = along(sums, 2, 0)
    for i, (_, size) in enumerate(chunks):
        width = packed_width(size, tok)
        updated = update(
            (*near, from_pair, from_opposite),
            ((0, offset),) * 5,
            packed[2 * i],
            packed[2 * i + 1],
            f"update_{i}",
        )
        handed.append(lax.ppermute(updated, "section", forward))
        offset += width
    return unpack(handed, tok, columns, chunks)[None]


def solution(mesh):
    placed = (
        P("section", "head", None, None),
        P("section", None, None, "head"),
        P("section", "head", None),
        P("section", "head", None),
        P("section", None),
        P("section"),
    )
    return jax.shard_map(
        shards, mesh=mesh, in_specs=placed, out_specs=P("section", "head", None), check_vma=False
    )
```

```python
import functools
import math

import jax
import jax.numpy as jnp
from jax import lax
from jax.experimental import pallas as pl
from jax.experimental.pallas import tpu as pltpu
from jax.sharding import PartitionSpec as P

HD = 128
CORES = 2
PAIR = 2
PLACES = ((0, 0), (0, 1), (1, 1), (3, 1), (1, 0), (3, 0), (2, 0), (2, 1))
MAIN = 16
SPLIT = (1, 2)
CHUNKS = 6
ATTEND_VMEM = 36 * 2**20
VMEM_LIMIT = 8 * 2**20


def in_vmem(x):
    return pltpu.with_memory_space_constraint(x, pltpu.VMEM)


def in_hbm(x):
    return pltpu.with_memory_space_constraint(x, pltpu.HBM)


def pack_kernel(qkv, out, in_s, rows_s, out_s, in_sems, out_sems, *, pieces):
    tok = qkv.shape[1]
    groups, _, width = out.shape
    part = tok // pieces
    step = groups // pieces_out(groups)
    arriving = []
    for n in range(pieces):
        rows = pl.ds(n * part, part)
        arriving.append(pltpu.make_async_copy(qkv.at[0, rows], in_s.at[rows], in_sems.at[n]))
        arriving[-1].start()
    for n in range(pieces):
        arriving[n].wait()
        for i in range(n * part, (n + 1) * part):
            value = in_s[i].astype(jnp.float32)
            for t in range(3):
                rows_s[t * tok + i : t * tok + i + 1, :] = value[t : t + 1]
    leaving = []
    for n in range(pieces_out(groups)):
        for g in range(n * step, (n + 1) * step):
            out_s[g] = rows_s[:, g * width : (g + 1) * width].astype(jnp.bfloat16)
        some = pl.ds(n * step, step)
        leaving.append(pltpu.make_async_copy(out_s.at[some], out.at[some], out_sems.at[n]))
        leaving[-1].start()
    for copy in leaving:
        copy.wait()


def pieces_out(groups):
    return 8 if groups % 8 == 0 else 1


def pack(qkv, groups):
    _, tok, _, columns = qkv.shape
    shape = (groups, 3 * tok, columns // groups)
    pieces = 6 if tok % 6 == 0 else 1
    anywhere = pl.BlockSpec(memory_space=pl.ANY)
    return pl.pallas_call(
        functools.partial(pack_kernel, pieces=pieces),
        in_specs=[anywhere],
        out_specs=anywhere,
        out_shape=pltpu.HBM(shape, jnp.bfloat16),
        scratch_shapes=[
            pltpu.VMEM((tok, 3, columns), jnp.bfloat16),
            pltpu.VMEM((3 * tok, columns), jnp.float32),
            pltpu.VMEM(shape, jnp.bfloat16),
            pltpu.SemaphoreType.DMA((pieces,)),
            pltpu.SemaphoreType.DMA((pieces_out(groups),)),
        ],
        compiler_params=pltpu.CompilerParams(vmem_limit_bytes=VMEM_LIMIT),
        name="pack",
    )(in_hbm(qkv))


def stream_kernel(residual, gate, *packed, chunks):
    rest = residual.shape[0] - MAIN
    cuts = MAIN // rest
    stream = residual[...].astype(jnp.float32)
    gates = gate[...]
    for i, (start, size) in enumerate(chunks):
        res_out, gate_out = packed[2 * i : 2 * i + 2]
        cut = size // cuts
        res_out[:, :size] = stream[:MAIN, start : start + size]
        gate_out[:, :size] = jnp.broadcast_to(gates[:, start : start + size], (MAIN, size))
        for b in range(cuts):
            cols = slice(start + b * cut, start + (b + 1) * cut)
            for t in range(rest):
                row = cuts * t + b
                res_out[row : row + 1, size:] = stream[MAIN + t : MAIN + t + 1, cols]
                gate_out[row : row + 1, size:] = gates[:, cols]


def stream(residual, gate, chunks):
    vmem = pl.BlockSpec(memory_space=pltpu.VMEM)
    packed = []
    for _, size in chunks:
        packed += [pltpu.VMEM((MAIN, packed_width(size, residual.shape[0])), jnp.float32)] * 2
    return pl.pallas_call(
        functools.partial(stream_kernel, chunks=chunks),
        in_specs=[vmem, vmem],
        out_specs=[vmem] * len(packed),
        out_shape=packed,
        compiler_params=pltpu.CompilerParams(vmem_limit_bytes=VMEM_LIMIT),
        name="stream",
    )(residual, gate)


def prefetch_kernel(kv, out, sems):
    copies = []
    for t in range(2):
        copies.append(pltpu.make_async_copy(kv.at[t, :, pl.ds(0, HD)], out.at[t], sems.at[t]))
        copies[-1].start()
    for copy in copies:
        copy.wait()


def prefetch(kv):
    return pl.pallas_call(
        prefetch_kernel,
        in_specs=[pl.BlockSpec(memory_space=pl.ANY)],
        out_specs=pl.BlockSpec(memory_space=pltpu.VMEM),
        out_shape=pltpu.VMEM((2, kv.shape[1], HD), kv.dtype),
        scratch_shapes=[pltpu.SemaphoreType.DMA((2,))],
        compiler_params=pltpu.CompilerParams(vmem_limit_bytes=2**20),
        name="prefetch",
    )(in_hbm(kv))


def attend_kernel(
    scalars, arrived, first_in, kv, w_keep, w_other,
    keep, send, w_out, first, q_s, fresh_s, sems, *kv_s, heads, chunk
):
    copies = []
    kv_s = (first.at[0], first.at[1]) + kv_s
    for h in range(1, heads):
        for t in range(2):
            n = 2 * (h - 1) + t
            copies.append(
                pltpu.make_async_copy(kv.at[t, :, pl.ds(h * HD, HD)], kv_s[2 * h + t], sems.at[n])
            )
    for i, w in enumerate((w_keep, w_other)):
        copies.append(pltpu.make_async_copy(w, w_out.at[i], sems.at[2 * heads - 2 + i]))
    for copy in copies:
        copy.start()
    groups = arrived.shape[0]
    tok = arrived.shape[1] // 3
    half = tok * groups // CORES
    peers = groups // CORES
    patch = tok * groups
    rest = tok - MAIN
    scale = math.log2(math.e) / math.sqrt(HD)
    core = lax.rem(scalars[1], CORES)
    here = lax.div(scalars[1], CORES)
    y_here, z_here = lax.div(here, PAIR), lax.rem(here, PAIR)
    for side in range(CORES):
        which = core if side == 0 else 1 - core
        for k, (dy, dz) in enumerate(PLACES):
            chip = lax.rem(y_here + dy, peers // PAIR) * PAIR + lax.rem(z_here + dz, PAIR)
            block = arrived[CORES * chip + which]
            for t in range(3):
                target = q_s if t == 0 else fresh_s.at[t - 1]
                rows = block[t * tok : (t + 1) * tok]
                target[pl.ds(side * half + MAIN * k, MAIN), :] = rows[:MAIN]
                target[pl.ds(side * half + MAIN * peers + rest * k, rest), :] = rows[MAIN:]
    own = pl.ds(pl.multiple_of(scalars[0] * patch, MAIN), patch)

    def ready(h, t):
        if h > 0:
            copies[2 * (h - 1) + t].wait()
        kv_s[2 * h + t][own, :] = fresh_s[t, :, h * HD : (h + 1) * HD]

    keys = kv_s[0].shape[0]
    for h in range(heads):
        ready(h, 0)
        ready(h, 1)
        cols = slice(h * HD, (h + 1) * HD)
        q = q_s[:, cols]

        def score(j):
            k = kv_s[2 * h][j * chunk : (j + 1) * chunk, :]
            return lax.dot_general(
                q, k, (((1,), (1,)), ((), ())), preferred_element_type=jnp.float32
            )

        top = total = acc = None
        upcoming = score(0)
        for j in range(keys // chunk):
            s = upcoming
            if j + 1 < keys // chunk:
                upcoming = score(j + 1)
            high = jnp.max(s, axis=1, keepdims=True)
            new_top = high if j == 0 else jnp.maximum(top, high)
            p = jnp.exp2((s - new_top) * scale)
            v = kv_s[2 * h + 1][j * chunk : (j + 1) * chunk, :]
            v = jnp.concatenate([v, jnp.ones_like(v)], axis=1)
            out = jnp.dot(p.astype(jnp.bfloat16), v, preferred_element_type=jnp.float32)
            out, part = out[:, :HD], out[:, HD:]
            if j == 0:
                total, acc = part, out
            else:
                fade = jnp.exp2((top - new_top) * scale)
                total = total * fade + part
                acc = acc * fade + out
            top = new_top
        done = (acc / total).astype(jnp.bfloat16)
        keep[:, cols] = done[:half]
        send[:, cols] = done[half:]
    for copy in copies[2 * heads - 2 :]:
        copy.wait()


def attend(scalars, arrived, first, kv, w_keep, w_other):
    groups, rows, width = arrived.shape
    keys = kv.shape[1]
    heads = width // HD
    patch = rows // 3 * groups
    result = pltpu.VMEM((patch // CORES, width), jnp.bfloat16)
    vmem = pl.BlockSpec(memory_space=pltpu.VMEM)
    anywhere = pl.BlockSpec(memory_space=pl.ANY)
    return pl.pallas_call(
        functools.partial(attend_kernel, heads=heads, chunk=keys // CHUNKS),
        in_specs=[pl.BlockSpec(memory_space=pltpu.SMEM), vmem, vmem] + [anywhere] * 3,
        out_specs=[vmem] * 4,
        out_shape=[
            result,
            result,
            pltpu.VMEM((CORES,) + w_keep.shape, w_keep.dtype),
            pltpu.VMEM(first.shape, first.dtype),
        ],
        scratch_shapes=[
            pltpu.VMEM((patch, width), jnp.bfloat16),
            pltpu.VMEM((2, patch, width), jnp.bfloat16),
            pltpu.SemaphoreType.DMA((2 * heads,)),
        ]
        + [pltpu.VMEM((keys, HD), jnp.bfloat16)] * (2 * heads - 2),
        input_output_aliases={2: 3},
        compiler_params=pltpu.CompilerParams(vmem_limit_bytes=ATTEND_VMEM),
        name="attend",
    )(scalars, in_vmem(arrived), in_vmem(first), *map(in_hbm, (kv, w_keep, w_other)))


def packed_width(size, tok):
    return size * tok // MAIN


def project_kernel(keep, other, weights, *refs, chunks):
    outs, rest_s = refs[:-1], refs[-1]
    peers = rest_s.shape[0]
    rest = keep.shape[0] // peers - MAIN
    cuts = MAIN // rest
    both = jnp.concatenate([keep[...], other[...]], axis=1)
    offset = 0
    for i, (start, size) in enumerate(chunks):
        cut = size // cuts
        width = size + cut
        span = pl.ds(offset, width)
        blocks = [ref.at[n, :, span] for ref in outs for n in range(ref.shape[0])]
        for b in range(cuts):
            cols = slice(start + b * cut, start + (b + 1) * cut)
            w = jnp.concatenate([weights[n, :, cols] for n in range(CORES)], axis=0)
            y = jnp.dot(both, w, preferred_element_type=jnp.float32)
            for d in range(peers):
                rows = y[MAIN * d : MAIN * (d + 1)]
                blocks[d][:, b * cut : (b + 1) * cut] = rows.astype(jnp.bfloat16)
                for t in range(rest):
                    row = MAIN * peers + rest * d + t
                    rest_s[d, cuts * t + b : cuts * t + b + 1, :cut] = y[row : row + 1]
        for d in range(peers):
            blocks[d][:, size:] = rest_s[d, :, :cut].astype(jnp.bfloat16)
        offset += width


def project(keep, other, weights, peers, chunks):
    rows, _ = keep.shape
    widths = [packed_width(size, rows // peers) for _, size in chunks]
    vmem = pl.BlockSpec(memory_space=pltpu.VMEM)
    shapes = [(1, MAIN, sum(widths))] * peers
    deepest = max(width - size for width, (_, size) in zip(widths, chunks))
    return pl.pallas_call(
        functools.partial(project_kernel, chunks=chunks),
        in_specs=[vmem] * 3,
        out_specs=[vmem] * len(shapes),
        out_shape=[pltpu.VMEM(shape, jnp.bfloat16) for shape in shapes],
        scratch_shapes=[pltpu.VMEM((peers, MAIN, deepest), jnp.float32)],
        compiler_params=pltpu.CompilerParams(vmem_limit_bytes=VMEM_LIMIT),
        name="project",
    )(in_vmem(keep), in_vmem(other), in_vmem(weights))


def total_of(refs, picks, width):
    total = None
    for ref, (n, offset) in zip(refs, picks):
        term = ref[n, :, offset : offset + width].astype(jnp.float32)
        total = term if total is None else total + term
    return total


def add_kernel(*refs, picks):
    out = refs[-1]
    out[0] = total_of(refs, picks, out.shape[2]).astype(jnp.bfloat16)


def add(arrays, after, picks, width, name):
    vmem = pl.BlockSpec(memory_space=pltpu.VMEM)
    return pl.pallas_call(
        functools.partial(add_kernel, picks=picks),
        in_specs=[vmem] * len(arrays) + [pl.BlockSpec(memory_space=pl.ANY)],
        out_specs=vmem,
        out_shape=pltpu.VMEM((1, MAIN, width), jnp.bfloat16),
        compiler_params=pltpu.CompilerParams(vmem_limit_bytes=VMEM_LIMIT),
        name=name,
    )(*map(in_vmem, arrays), after)


def update_kernel(*refs, picks):
    residual, gate, out = refs[-3:]
    total = total_of(refs, picks, out.shape[1])
    out[...] = (residual[...] + gate[...] * total).astype(jnp.bfloat16)


def update(arrays, picks, residual, gate, name):
    vmem = pl.BlockSpec(memory_space=pltpu.VMEM)
    return pl.pallas_call(
        functools.partial(update_kernel, picks=picks),
        in_specs=[vmem] * (len(arrays) + 2),
        out_specs=vmem,
        out_shape=pltpu.VMEM(residual.shape, jnp.bfloat16),
        compiler_params=pltpu.CompilerParams(vmem_limit_bytes=VMEM_LIMIT),
        name=name,
    )(*map(in_vmem, (*arrays, residual, gate)))


def unpack_kernel(*refs, chunks):
    out = refs[-1]
    rest = out.shape[0] - MAIN
    cuts = MAIN // rest
    for packed, (start, size) in zip(refs, chunks):
        cut = size // cuts
        out[0:MAIN, start : start + size] = packed[:, :size]
        tail = packed[:, size:].astype(jnp.float32)
        for b in range(cuts):
            pieces = [tail[cuts * t + b : cuts * t + b + 1] for t in range(rest)]
            cols = slice(start + b * cut, start + (b + 1) * cut)
            out[MAIN:, cols] = jnp.concatenate(pieces, axis=0).astype(jnp.bfloat16)


def unpack(packed, rows, columns, chunks):
    vmem = pl.BlockSpec(memory_space=pltpu.VMEM)
    return pl.pallas_call(
        functools.partial(unpack_kernel, chunks=chunks),
        in_specs=[vmem] * len(packed),
        out_specs=vmem,
        out_shape=jax.ShapeDtypeStruct((rows, columns), jnp.bfloat16),
        compiler_params=pltpu.CompilerParams(vmem_limit_bytes=VMEM_LIMIT),
        name="unpack",
    )(*map(in_vmem, packed))


def shards(qkv, stale_kv, out_weight, residual, gate, patch_of_section):
    groups = lax.axis_size("head")
    sections = lax.axis_size("section")
    peers = groups // CORES
    tok = qkv.shape[1]
    columns = out_weight.shape[2]
    swap = [(i, i ^ 1) for i in range(groups)]
    chunks = []
    for parts in SPLIT:
        start = sum(size for _, size in chunks)
        chunks.append((start, columns * parts // sum(SPLIT)))

    scalars = jnp.stack([patch_of_section[0], lax.axis_index("head").astype(jnp.int32)])
    weight = out_weight[0]
    weight_other = lax.ppermute(weight, "head", swap)
    blocked = pack(qkv, groups)
    arrived = lax.all_to_all(blocked, "head", split_axis=0, concat_axis=0, tiled=True)
    kv = jnp.transpose(stale_kv[0], (1, 0, 2))

    keep, send, weights, _ = attend(scalars, arrived, prefetch(kv), kv, weight, weight_other)
    other = lax.ppermute(send, "head", swap)
    packed = stream(residual[0], gate, chunks)
    forward = [(j, (j + 1) % sections) for j in range(sections)]

    def along(x, dy, dz):
        route = [(i, (i + dy * PAIR * CORES) % groups ^ dz * CORES) for i in range(groups)]
        return lax.ppermute(x, "head", route)

    mine, pair, ahead_far, behind_far, ahead, behind, opposite, across = project(
        keep, other, weights, peers, chunks
    )
    far = (pair, along(ahead_far, 1, 0), along(behind_far, -1, 0))
    across = along(across, 0, 1)
    near = (mine, along(ahead, 1, 0), along(behind, -1, 0))
    handed = []
    turn = keep
    offset = 0
    width = mine.shape[2]
    sums = add(far, keep, ((0, 0),) * 3, width, "pair")
    from_pair = along(sums, 0, 1)
    sums = add((opposite, across), sums, ((0, 0),) * 2, width, "opposite")
    from_opposite = along(sums, 2, 0)
    for i, (_, size) in enumerate(chunks):
        width = packed_width(size, tok)
        updated = update(
            (*near, from_pair, from_opposite),
            ((0, offset),) * 5,
            packed[2 * i],
            packed[2 * i + 1],
            f"update_{i}",
        )
        handed.append(lax.ppermute(updated, "section", forward))
        offset += width
    return unpack(handed, tok, columns, chunks)[None]


def solution(mesh):
    placed = (
        P("section", "head", None, None),
        P("section", None, None, "head"),
        P("section", "head", None),
        P("section", "head", None),
        P("section", None),
        P("section"),
    )
    return jax.shard_map(
        shards, mesh=mesh, in_specs=placed, out_specs=P("section", "head", None), check_vma=False
    )
```
